256 devices in a mesh: factor: 16 (over x_hi, z), col: 16 (over x_lo, y, core).
Axes of the slice: x: 4 (x_hi: 2, x_lo: 2; x = x_hi * 2 + x_lo), y: 4, z: 8, core: 2. Of those that a mesh axis runs over, the one named last changes fastest.
Arguments:
- activations: bfloat16 [16384, 2048], P('factor', 'col'), may hold values from -2.5 to 2.5
- targets: bfloat16 [16384, 2048], P('factor', 'col'), may hold values from -6 to 6
- diagonal: float32 [14, 16384], P(None, 'factor'), may hold values from 0.6 to 0.8
- crossing: float32 [14, 16384], P(None, 'factor'), may hold values from -2.5 to 2.5
Outputs:
- new_diagonal: float32 [14, 16384], P(None, 'factor')
- new_crossing: float32 [14, 16384], P(None, 'factor')
- residual: float32 [16384, 2048], P('factor', 'col')
The draws below stay inside these ranges and needn't reach their ends.
All inputs are finite; a program needn't handle non-finite values.
Results may differ from the reference program's by a relative error of at most 0.0003.
Values sent between devices are 32-bit elements; how exact they have to be, the bound alone decides.
A program may use at most 64 MiB of HBM per device.

```python
import jax
import jax.numpy as jnp
from jax import lax

D = 16384
SECTIONS = 14
TOK_DEV = 128
ITERS = 1
TOKENS = 2048


def block_scale(key, shape, pieces, least, largest):
    loudness, own = 1.0, jax.random.fold_in(key, 6)
    for position, parts in pieces:
        draws = jnp.exp(jax.random.uniform(jax.random.fold_in(own, position), (parts,), jnp.float32, least / len(pieces), largest / len(pieces)))
        loudness = loudness * jnp.repeat(draws, shape[position] // parts).reshape([-1 if axis == position else 1 for axis in range(len(shape))])
    return loudness


def bell_draw(own_key, dims, scale, most, shards=(), held_as=jnp.bfloat16):
    level = block_scale(own_key, dims, shards, -0.22, 0.18) if shards else 1.0
    result = jax.random.normal(own_key, dims, jnp.float32) * scale * level
    return jnp.minimum(jnp.maximum(result, -most), most).astype(held_as)


def setup_inputs(seed: int = 0) -> dict:
    keys = jax.random.split(jax.random.key(seed), 5)
    return {
        "activations": bell_draw(keys[0], (D, TOKENS), 1.0, 2.5, ((0, 16), (1, 16))),
        "targets": bell_draw(keys[1], (D, TOKENS), 1.0, 6.0, ((0, 16), (1, 16))),
        "diagonal": jnp.clip(0.6 + 0.19999999 * jax.random.uniform(keys[2], (SECTIONS, D), jnp.float32) ** block_scale(keys[2], (SECTIONS, D), ((1, 16),), -0.2, 0.2), 0.6, 0.8),
        "crossing": bell_draw(keys[3], (SECTIONS, D), 0.7, 2.5, ((1, 16),), jnp.float32),
    }


step_scale = 0.03

def section_mix(field, diagonal_row, crossing_row, level):
    stride = 2 ** level
    folded = field.reshape(D // (2 * stride), 2, stride, field.shape[1])
    beside = jnp.flip(folded, 1).reshape(field.shape)
    return diagonal_row[:, None] * field + crossing_row[:, None] * beside

def reverse_rows(field):
    count = field.shape[1]
    axes = tuple(range(SECTIONS - 1, -1, -1)) + (SECTIONS,)
    return jnp.transpose(field.reshape((2,) * SECTIONS + (count,)), axes).reshape(D, count)

def forward(diagonal, crossing, block):
    field = block.astype(jnp.float32)
    for level in range(SECTIONS):
        field = section_mix(field, diagonal[level], crossing[level], level)
    return reverse_rows(field)

def reference(activations, targets, diagonal, crossing):
    blocks = TOKENS // TOK_DEV
    act_blocks = activations.reshape(D, blocks, TOK_DEV).transpose(1, 0, 2)
    goal_blocks = targets.reshape(D, blocks, TOK_DEV).transpose(1, 0, 2)
    residual = None
    for step in range(ITERS):

        def visit(carry, pair, diagonal=diagonal, crossing=crossing):
            block, goal = pair
            output, pull = jax.vjp(lambda left, right: forward(left, right, block), diagonal, crossing)
            error = output - goal.astype(jnp.float32)
            grad_left, grad_right = pull(2.0 / TOKENS * error)
            return ((carry[0] + grad_left, carry[1] + grad_right), error)
        zeros = jnp.zeros_like(diagonal)
        sums, errors = lax.scan(visit, (zeros, zeros), (act_blocks, goal_blocks))
        diagonal = diagonal - step_scale * sums[0]
        crossing = crossing - step_scale * sums[1]
        residual = errors.transpose(1, 0, 2).reshape(D, TOKENS)
    return (diagonal, crossing, residual)
```

```python
import functools

import jax
import jax.numpy as jnp
from jax import lax
from jax.experimental import pallas as pl
from jax.experimental.pallas import tpu as pltpu
from jax.sharding import PartitionSpec as P

MESH = pl.DeviceIdType.MESH
F32, BF16 = jnp.float32, jnp.bfloat16
step_scale = 0.03
TOKENS = 2048


def bit(value, place):
    return lax.rem(lax.div(value, 2**place), 2)


def rev3(v):
    return bit(v, 0) * 4 + bit(v, 1) * 2 + bit(v, 2)


def rev4(v):
    return bit(v, 0) * 8 + bit(v, 1) * 4 + bit(v, 2) * 2 + bit(v, 3)


def rev_const(v, bits):
    return int(format(v, "0%db" % bits)[::-1], 2)


def flip(value, place):
    return value + 2**place - 2 ** (place + 1) * bit(value, place)


def forward_pairs(x, span, diag, cross):
    out = list(x)
    for i in range(len(x)):
        out[i] = diag(i) * x[i] + cross(i) * x[i ^ span]
    return out


def backward_pairs(b, span, diag, cross):
    carried = [cross(i) * b[i] for i in range(len(b))]
    return [diag(i) * b[i] + carried[i ^ span] for i in range(len(b))]


def loop(count, body):
    def step(j, carry):
        body(j)
        return carry

    lax.fori_loop(0, count, step, 0)


def lane_sums(pairs):
    rows = lax.broadcasted_iota(jnp.int32, (16, 128), 0)
    total = None
    for level, (first, second) in enumerate(pairs):
        ones = jnp.where(rows == level, 1.0, 0.0).astype(BF16)
        block = jnp.concatenate([first, second], axis=0)
        high = block.astype(BF16)
        low = (block - high.astype(F32)).astype(BF16)
        for part in (high, low):
            term = lax.dot_general(ones, part, (((1,), (1,)), ((), ())), preferred_element_type=F32)
            total = term if total is None else total + term
    return total


def swap_tiles(block, span):
    tiles = [block[8 * k : 8 * k + 8] for k in range(8)]
    return jnp.concatenate([tiles[k ^ span] for k in range(8)], axis=0)


def kernel(
    act, tgt, dg, cr,
    nd, nc, res,
    xs, ts, wst, wt, wts, wz, wmsg, wbin, wtb,
    wa, wb, fa, ba, fb, bb,
    inb, outb, ina, ga, gb, gpart, gsum, rs, ot, pt,
    s1, r1, s2, r2, s3, r3, s4, r4, s5, r5, s6, r6,
):
    me = lax.axis_index("factor")
    col = lax.axis_index("col")
    mx, mz = lax.div(me, 8), lax.rem(me, 8)

    barrier = pltpu.get_barrier_semaphore()

    def greet(j):
        pl.semaphore_signal(
            barrier, inc=1, device_id={"factor": lax.rem(me + 1 + j, 16)}, device_id_type=MESH
        )
        pl.semaphore_signal(
            barrier, inc=1, device_id={"col": lax.rem(col + 1 + j, 16)}, device_id_type=MESH
        )

    loop(15, greet)

    def peer(j, sign):
        dx = 1 - lax.div(j, 8)
        dz = lax.rem(dx * (j + 4) + (1 - dx) * (j - 7), 8)
        return lax.rem(mx + dx, 2) * 8 + lax.rem(mz + sign * dz + 8, 8)

    wst[...] = jnp.zeros_like(wst)
    for s in range(14):
        row = s + (s >= 7)
        wst[row : row + 1, :] = dg[s : s + 1, :]
        wst[16 + row : 17 + row, :] = cr[s : s + 1, :]
    for k in range(8):
        wt[128 * k : 128 * k + 128, :] = wst[:, 128 * k : 128 * k + 128].T

    def spread_a(u):
        t = rev3(u)
        here = pl.ds(8 * u, 8)
        for a in range(16):
            tile = wt[pl.ds(16 * t + a, 8, stride=128), :]
            wts[a, here, :] = tile
            for s in range(7):
                wa[0, s, a, here, :] = jnp.broadcast_to(tile[:, s : s + 1], (8, 128))
                wa[1, s, a, here, :] = jnp.broadcast_to(tile[:, 16 + s : 17 + s], (8, 128))

    loop(8, spread_a)

    lane = lax.broadcasted_iota(jnp.int32, (8, 128), 1)

    def pack_b(p):
        for kind in range(2):
            packed = jnp.zeros((8, 128), F32)
            for a in range(16):
                tile = wts[a, pl.ds(p, 8, stride=8), :]
                moved = pltpu.roll(tile, (8 * a - 8 - 16 * kind) % 128, axis=1)
                packed = jnp.where(lax.div(lane, 8) == a, moved, packed)
            wz[pl.ds(64 * kind + 8 * p, 8), :] = packed

    loop(8, pack_b)
    wmsg[...] = wz[...].T.reshape(16, 8, 128)

    def convert(j):
        here = pl.ds(16 * j, 16)
        xs[here, :] = act[here, :].astype(F32)
        ts[here, :] = tgt[here, :].astype(F32)

    loop(64, convert)

    def forward_a(u):
        t = rev3(u)
        here = pl.ds(8 * u, 8)
        x = [xs[pl.ds(16 * t + a, 8, stride=128), :] for a in range(16)]
        for s in range(4):
            for a in range(16):
                fa[s, a, here, :] = x[a]
            x = forward_pairs(x, 2**s, lambda a: wa[0, s, a, here, :], lambda a: wa[1, s, a, here, :])
        for a in range(16):
            fa[4, a, here, :] = x[a]

    loop(8, forward_a)

    def tile(k):
        return slice(8 * k, 8 * k + 8)

    def finish_a(a, target, index):
        x = [fa[4, a, tile(u), :] for u in range(8)]
        for s in range(4, 7):
            if s > 4:
                for u in range(8):
                    fa[s, a, tile(u), :] = x[u]
            x = forward_pairs(
                x, 2 ** (6 - s), lambda u: wa[0, s, a, tile(u), :], lambda u: wa[1, s, a, tile(u), :]
            )
        for u in range(8):
            target[index, tile(u), :] = x[u]

    pl.semaphore_wait(barrier, 30)

    def copy_w(g):
        return pltpu.make_async_remote_copy(
            src_ref=wmsg.at[rev4(g)], dst_ref=wbin.at[me], send_sem=s1.at[g], recv_sem=r1.at[me],
            device_id={"factor": g}, device_id_type=MESH,
        )

    def copy_x(g):
        return pltpu.make_async_remote_copy(
            src_ref=outb.at[rev4(g)], dst_ref=inb.at[me], send_sem=s2.at[g], recv_sem=r2.at[me],
            device_id={"factor": g}, device_id_type=MESH,
        )

    def landed(buffer, sems, source):
        return pltpu.make_async_remote_copy(
            src_ref=buffer.at[source], dst_ref=buffer.at[source], send_sem=sems.at[source], recv_sem=sems.at[source],
            device_id={"factor": source}, device_id_type=MESH,
        ).wait_recv()

    def send_a(j):
        g = peer(j, 1)
        copy_w(g).start()
        finish_a(rev4(g), outb, rev4(g))
        copy_x(g).start()

    loop(15, send_a)
    finish_a(rev4(me), inb, me)
    wbin[me] = wmsg[rev4(me)]

    loop(15, lambda j: landed(wbin, r1, peer(j, -1)))
    wtb[...] = wbin[...].reshape(128, 128).T

    def spread_b(p):
        here = pl.ds(8 * p, 8)
        diag = wtb[here, :]
        cross = wtb[pl.ds(64 + 8 * p, 8), :]
        for f in range(16):
            for s in range(7):
                k = 8 * f + s
                wb[0, s, f, here, :] = jnp.broadcast_to(diag[:, k : k + 1], (8, 128))
                wb[1, s, f, here, :] = jnp.broadcast_to(cross[:, k : k + 1], (8, 128))

    loop(8, spread_b)

    def forward_b(f):
        x = [inb[f, pl.ds(p, 8, stride=8), :] for p in range(8)]
        for s in range(3):
            for p in range(8):
                fb[s, f, tile(p), :] = x[p]
            x = forward_pairs(x, 2**s, lambda p: wb[0, s, f, tile(p), :], lambda p: wb[1, s, f, tile(p), :])
        for p in range(8):
            fb[3, f, tile(p), :] = x[p]

    forward_b(me)

    def arrive_b(j):
        f = peer(14 - j, -1)
        landed(inb, r2, f)
        forward_b(f)

    loop(15, arrive_b)

    def turn(p):
        here = pl.ds(8 * p, 8)
        x = [fb[3, f, here, :] for f in range(16)]
        for s in range(3, 7):
            if s > 3:
                for f in range(16):
                    fb[s, f, here, :] = x[f]
            x = forward_pairs(x, 2 ** (s - 3), lambda f: wb[0, s, f, here, :], lambda f: wb[1, s, f, here, :])
        b = []
        for f in range(16):
            rows = pl.ds(rev3(p) * 16 + rev_const(f, 4), 8, stride=128)
            error = x[f] - ts[rows, :]
            res[rows, :] = error
            b.append((2.0 / TOKENS) * error)
        for s in range(6, 2, -1):
            for f in range(16):
                bb[s, f, here, :] = b[f]
            b = backward_pairs(b, 2 ** (s - 3), lambda f: wb[0, s, f, here, :], lambda f: wb[1, s, f, here, :])
        for f in range(16):
            bb[2, f, here, :] = b[f]

    loop(8, turn)

    def backward_b(f, target, index):
        b = [bb[2, f, tile(p), :] for p in range(8)]
        for s in range(2, -1, -1):
            if s < 2:
                for p in range(8):
                    bb[s, f, tile(p), :] = b[p]
            b = backward_pairs(b, 2**s, lambda p: wb[0, s, f, tile(p), :], lambda p: wb[1, s, f, tile(p), :])
        for p in range(8):
            target[index, pl.ds(p, 8, stride=8), :] = b[p]

    loop(15, lambda j: copy_x(peer(j, 1)).wait_send())
    mine = rev4(me)

    def copy_b(f):
        return pltpu.make_async_remote_copy(
            src_ref=outb.at[f], dst_ref=ina.at[mine], send_sem=s3.at[f], recv_sem=r3.at[mine],
            device_id={"factor": f}, device_id_type=MESH,
        )

    def send_b(j):
        f = peer(j, 1)
        backward_b(f, outb, f)
        copy_b(f).start()

    loop(15, send_b)
    backward_b(me, ina, mine)

    def grads_b(f):
        pairs = []
        for s in range(7):
            back = bb[s, f]
            own = fb[s, f]
            other = swap_tiles(own, 2**s) if s < 3 else fb[s, flip(f, s - 3)]
            pairs.append((back * own, back * other))
        return lane_sums(pairs)[0:8]

    def copy_g(f):
        return pltpu.make_async_remote_copy(
            src_ref=gb.at[f], dst_ref=gpart.at[1, mine], send_sem=s4.at[f], recv_sem=r4.at[mine],
            device_id={"factor": f}, device_id_type=MESH,
        )

    def send_g(j):
        f = peer(j, 1)
        gb[f] = grads_b(f)
        copy_g(f).start()

    loop(15, send_g)
    gpart[1, mine] = grads_b(me)

    def backward_a(a):
        b = [ina[a, tile(u), :] for u in range(8)]
        for s in range(6, 3, -1):
            for u in range(8):
                ba[s, a, tile(u), :] = b[u]
            b = backward_pairs(
                b, 2 ** (6 - s), lambda u: wa[0, s, a, tile(u), :], lambda u: wa[1, s, a, tile(u), :]
            )
        for u in range(8):
            ba[3, a, tile(u), :] = b[u]

    backward_a(mine)

    def arrive_a(j):
        g = peer(14 - j, -1)
        a = rev4(g)
        landed(ina, r3, a)
        backward_a(a)

    loop(15, arrive_a)

    def last_a(u):
        here = pl.ds(8 * u, 8)
        b = [ba[3, a, here, :] for a in range(16)]
        for s in range(3, 0, -1):
            b = backward_pairs(b, 2**s, lambda a: wa[0, s, a, here, :], lambda a: wa[1, s, a, here, :])
            for a in range(16):
                ba[s - 1, a, here, :] = b[a]

    loop(8, last_a)

    def grads_a(a):
        pairs = []
        for s in range(7):
            back = ba[s, a]
            own = fa[s, a]
            other = fa[s, flip(a, s)] if s < 4 else swap_tiles(own, 2 ** (6 - s))
            pairs.append((back * own, back * other))
        gpart[0, a] = lane_sums(pairs)[0:8]

    loop(16, grads_a)

    def landed_g(j):
        a = rev4(peer(j, -1))
        pltpu.make_async_remote_copy(
            src_ref=gb.at[a], dst_ref=gpart.at[1, a], send_sem=s4.at[a], recv_sem=r4.at[a],
            device_id={"factor": me}, device_id_type=MESH,
        ).wait_recv()

    loop(15, landed_g)

    def copy_r(c):
        return pltpu.make_async_remote_copy(
            src_ref=gpart.at[:, c], dst_ref=rs.at[col], send_sem=s5.at[c], recv_sem=r5.at[col],
            device_id={"col": c}, device_id_type=MESH,
        )

    def col_landed(buffer, sems, source):
        pltpu.make_async_remote_copy(
            src_ref=buffer, dst_ref=buffer, send_sem=sems.at[source], recv_sem=sems.at[source],
            device_id={"col": source}, device_id_type=MESH,
        ).wait_recv()

    loop(15, lambda j: copy_r(lax.rem(col + 1 + j, 16)).start())
    rs[col] = gpart[:, col]
    loop(15, lambda j: col_landed(rs.at[lax.rem(col + 15 - j, 16)], r5, lax.rem(col + 15 - j, 16)))
    summed = rs[0]
    for c in range(1, 16):
        summed = summed + rs[c]
    gsum[:, col] = summed

    def copy_s(c):
        return pltpu.make_async_remote_copy(
            src_ref=gsum.at[:, col], dst_ref=gsum.at[:, col], send_sem=s6.at[c], recv_sem=r6.at[col],
            device_id={"col": c}, device_id_type=MESH,
        )

    loop(15, lambda j: copy_s(lax.rem(col + 1 + j, 16)).start())
    loop(15, lambda j: col_landed(gsum.at[:, lax.rem(col + 15 - j, 16)], r6, lax.rem(col + 15 - j, 16)))

    pt[0] = gsum[0].reshape(128, 128).T
    pt[1] = gsum[1].reshape(128, 128).T

    def unpack(u):
        t = rev3(u)
        parts = []
        for kind in range(2):
            parts.append(pt[0, pl.ds(64 * kind + 8 * u, 8), :])
            parts.append(pt[1, pl.ds(64 * kind + u, 8, stride=8), :])
        for a in range(16):
            row = jnp.zeros((8, 128), F32)
            for k in range(4):
                row = jnp.where(lax.div(lane, 8) == k, pltpu.roll(parts[k], (8 * k - 8 * a) % 128, axis=1), row)
            ot[pl.ds(16 * t + a, 8, stride=128), :] = row

    loop(8, unpack)
    for k in range(8):
        here = slice(128 * k, 128 * k + 128)
        wst[:, here] = ot[here, :].T
    for s in range(14):
        row = s + (s >= 7)
        nd[s : s + 1, :] = dg[s : s + 1, :] - step_scale * wst[row : row + 1, :]
        nc[s : s + 1, :] = cr[s : s + 1, :] - step_scale * wst[16 + row : 17 + row, :]

    def drain(j):
        g = peer(j, 1)
        copy_w(g).wait_send()
        copy_b(g).wait_send()
        copy_g(g).wait_send()
        c = lax.rem(col + 1 + j, 16)
        copy_r(c).wait_send()
        copy_s(c).wait_send()

    loop(15, drain)


def per_device(activations, targets, diagonal, crossing):
    height, width = activations.shape
    big = lambda *lead: pltpu.VMEM(lead + (16, 64, 128), F32)
    plain = lambda *shape: pltpu.VMEM(shape, F32)
    return pl.pallas_call(
        kernel,
        out_shape=(
            jax.ShapeDtypeStruct(diagonal.shape, F32),
            jax.ShapeDtypeStruct(crossing.shape, F32),
            jax.ShapeDtypeStruct((height, width), F32),
        ),
        in_specs=[pl.BlockSpec(memory_space=pltpu.VMEM)] * 4,
        out_specs=(pl.BlockSpec(memory_space=pltpu.VMEM),) * 3,
        scratch_shapes=[
            plain(1024, 128), plain(1024, 128), plain(128, 1024), plain(1024, 128), plain(16, 64, 128),
            plain(128, 128), plain(16, 8, 128), plain(16, 8, 128), plain(128, 128),
            big(2, 7), big(2, 7), big(7), big(7), big(7), big(7),
            big(), big(), big(), plain(16, 8, 128), plain(16, 8, 128),
            plain(2, 16, 8, 128), plain(2, 16, 8, 128), plain(16, 2, 8, 128), plain(1024, 128), plain(2, 128, 128),
        ]
        + [pltpu.SemaphoreType.DMA((16,))] * 12,
        compiler_params=pltpu.CompilerParams(
            collective_id=0, has_side_effects=True, vmem_limit_bytes=56 * 2**20
        ),
    )(activations, targets, diagonal, crossing)


def solution(mesh):
    placed = (P("factor", "col"), P("factor", "col"), P(None, "factor"), P(None, "factor"))
    return jax.shard_map(
        per_device,
        mesh=mesh,
        in_specs=placed,
        out_specs=(P(None, "factor"), P(None, "factor"), P("factor", "col")),
        check_vma=False,
    )
```

```python
import jax
import jax.numpy as jnp
from jax import lax
from jax.experimental import pallas as pl
from jax.experimental.pallas import tpu as pltpu
from jax.sharding import PartitionSpec as P

MESH = pl.DeviceIdType.MESH
F32, BF16 = jnp.float32, jnp.bfloat16
step_scale = 0.03
TOKENS = 2048
PARTS = 4
UP = 8 // PARTS


def bit(value, place):
    return lax.rem(lax.div(value, 2**place), 2)


def rev3(v):
    return bit(v, 0) * 4 + bit(v, 1) * 2 + bit(v, 2)


def rev4(v):
    return bit(v, 0) * 8 + bit(v, 1) * 4 + bit(v, 2) * 2 + bit(v, 3)


def rev_const(v, bits):
    return int(format(v, "0%db" % bits)[::-1], 2)


def slot(s):
    return s + (s >= 3)


def forward_pairs(x, span, diag, cross):
    return [diag(i) * x[i] + cross(i) * x[i ^ span] for i in range(len(x))]


def backward_pairs(b, span, diag, cross):
    carried = [cross(i) * b[i] for i in range(len(b))]
    return [diag(i) * b[i] + carried[i ^ span] for i in range(len(b))]


def loop(count, body):
    def step(j, carry):
        body(j)
        return carry

    lax.fori_loop(0, count, step, 0)


def thirds(value):
    high = value.astype(BF16).astype(F32)
    rest = value - high
    middle = rest.astype(BF16).astype(F32)
    return high, middle, rest - middle


def kernel(
    act_hbm, tgt_hbm, dg_hbm, cr_hbm,
    nd, nc, res,
    act, tgt, dg, cr,
    xs, ts, es, wst, wt, wtb16, ebc, wz, wmsg, wbin, wtb,
    wa, w1, w2, fa, b5, f1, f2, b1, b2,
    outa, inb, outb, ina, parta, partb, gz, gt, gin, gpart, rs, gs, gout,
    ld, s1, r1, s2, r2, s3, r3, s4, r4, s5, r5, s6, r6,
):
    me = lax.axis_index("factor")
    col = lax.axis_index("col")
    mx, mz = lax.div(me, 8), lax.rem(me, 8)
    mine = rev4(me)

    loads = [
        pltpu.make_async_copy(a, b, ld.at[k])
        for k, (a, b) in enumerate([(dg_hbm, dg), (cr_hbm, cr), (act_hbm, act), (tgt_hbm, tgt)])
    ]
    for copy in loads:
        copy.start()

    barrier = pltpu.get_barrier_semaphore()

    def greet(j):
        pl.semaphore_signal(
            barrier, inc=1, device_id={"factor": lax.rem(me + 1 + j, 16)}, device_id_type=MESH
        )
        pl.semaphore_signal(
            barrier, inc=1, device_id={"col": lax.rem(col + 1 + j, 16)}, device_id_type=MESH
        )

    loop(15, greet)

    def peer(j, sign):
        dx = 1 - lax.div(j, 8)
        dz = lax.rem(dx * (j + 4) + (1 - dx) * (j - 7), 8)
        return lax.rem(mx + dx, 2) * 8 + lax.rem(mz + sign * dz + 8, 8)

    lane = lax.broadcasted_iota(jnp.int32, (8, 128), 1)
    lane_low = [lax.rem(lax.div(lane, 2**k), 2) == 0 for k in range(7)]

    def choose(tiles):
        k = 3
        while len(tiles) > 1:
            tiles = [jnp.where(lane_low[k], tiles[i], tiles[i + 1]) for i in range(0, len(tiles), 2)]
            k += 1
        return tiles[0]

    def lane_sums(blocks, n):
        block = jnp.concatenate(blocks, axis=0)
        high = block.astype(BF16)
        low = (block - high.astype(F32)).astype(BF16)
        return jnp.dot(jnp.concatenate([high, low], axis=1), ebc[n], preferred_element_type=F32)

    def tiles_of(block, k):
        return [block[128 * k + 8 * i : 128 * k + 8 * i + 8] for i in range(16)]

    wst[96:128, :] = jnp.zeros((32, 1024), F32)
    loads[0].wait()
    loads[1].wait()
    for s in range(14):
        row = 96 + (s if s < 7 else 8 + slot(s - 7))
        wst[row : row + 1, :] = dg[s : s + 1, :]
        wst[16 + row : 17 + row, :] = cr[s : s + 1, :]
    high, middle, rest = thirds(wst[96:128, :])
    wst[0:32, :] = high
    wst[32:64, :] = middle
    wst[64:96, :] = rest
    for k in range(8):
        wt[128 * k : 128 * k + 128, :] = wst[:, 128 * k : 128 * k + 128].T

    def gather_a(w):
        for a in range(16):
            tiles = [wt[pl.ds(16 * rev3(2 * w + k) + a, 8, stride=128), :] for k in range(2)]
            wtb16[pl.ds(64 * a + 16 * w, 16), :] = jnp.concatenate(tiles, axis=0).astype(BF16)

    loop(4, gather_a)

    def spread_a(s):
        rows = lax.broadcasted_iota(jnp.int32, (128, 256), 0)
        kind = lax.div(lax.broadcasted_iota(jnp.int32, (128, 256), 1), 128)
        chosen = (lax.rem(rows, 32) == 16 * kind + s) & (rows < 96)
        ones = jnp.where(chosen, 1.0, 0.0).astype(BF16)
        for half in range(4):
            r = jnp.dot(wtb16[256 * half : 256 * half + 256, :], ones, preferred_element_type=F32)
            wa[0, s, 4 * half : 4 * half + 4] = r[:, :128].reshape(4, 64, 128)
            wa[1, s, 4 * half : 4 * half + 4] = r[:, 128:].reshape(4, 64, 128)

    loop(7, spread_a)

    loads[2].wait()

    def convert(j):
        here = pl.ds(16 * j, 16)
        xs[here, :] = act[here, :].astype(F32)

    loop(64, convert)

    def forward_a(u):
        t = rev3(u)
        here = pl.ds(8 * u, 8)
        x = [xs[pl.ds(16 * t + a, 8, stride=128), :] for a in range(16)]
        for s in range(4):
            for a in range(16):
                fa[s, a, here, :] = x[a]
            x = forward_pairs(x, 2**s, lambda a: wa[0, s, a, here, :], lambda a: wa[1, s, a, here, :])
        for a in range(16):
            fa[4, a, here, :] = x[a]

    loop(8, forward_a)

    def tile(k):
        return slice(8 * k, 8 * k + 8)

    def finish_a(a):
        x = [fa[4, a, tile(u), :] for u in range(8)]
        for s in range(4, 7):
            if s > 4:
                for u in range(8):
                    fa[s, a, tile(u), :] = x[u]
            x = forward_pairs(
                x, 2 ** (6 - s), lambda u: wa[0, s, a, tile(u), :], lambda u: wa[1, s, a, tile(u), :]
            )
        for u in range(8):
            outa[a, tile(u), :] = x[u]

    loop(16, finish_a)

    pl.semaphore_wait(barrier, 30)

    def copy_w(g):
        return pltpu.make_async_remote_copy(
            src_ref=wmsg.at[rev4(g)], dst_ref=wbin.at[me], send_sem=s1.at[g], recv_sem=r1.at[me],
            device_id={"factor": g}, device_id_type=MESH,
        )

    def copy_x(g, w):
        return pltpu.make_async_remote_copy(
            src_ref=outa.at[rev4(g), pl.ds(8 * UP * w, 8 * UP)], dst_ref=inb.at[w, pl.ds(8 * UP * me, 8 * UP)],
            send_sem=s2.at[w, g], recv_sem=r2.at[w, me], device_id={"factor": g}, device_id_type=MESH,
        )

    def arrived(place, sem, axis, source):
        pltpu.make_async_remote_copy(
            src_ref=place, dst_ref=place, send_sem=sem, recv_sem=sem, device_id={axis: source}, device_id_type=MESH
        ).wait_recv()

    loop(15, lambda j: copy_x(peer(j, 1), 0).start())

    def pack_w(u):
        t = rev3(u)
        packed = [jnp.zeros((8, 128), F32) for kind in range(2)]
        for a in range(16):
            rows = wt[pl.ds(16 * t + a, 8, stride=128), :]
            for kind in range(2):
                moved = pltpu.roll(rows, (8 * a - 104 - 16 * kind) % 128, axis=1)
                packed[kind] = jnp.where(lax.div(lane, 8) == a, moved, packed[kind])
        for kind in range(2):
            wz[pl.ds(64 * kind + u, 8, stride=8), :] = packed[kind]

    loop(8, pack_w)
    wmsg[...] = wz[...].T.reshape(16, 8, 128)
    loop(15, lambda j: copy_w(peer(j, 1)).start())
    for w in range(1, PARTS):
        loop(15, lambda j: copy_x(peer(j, 1), w).start())
    wbin[me] = wmsg[mine]
    for w in range(PARTS):
        inb[w, pl.ds(8 * UP * me, 8 * UP), :] = outa[mine, 8 * UP * w : 8 * UP * w + 8 * UP, :]

    def column_ones(n):
        chosen = lax.rem(lax.broadcasted_iota(jnp.int32, (256, 128), 1), 8) == n
        ebc[n] = jnp.where(chosen, 1.0, 0.0).astype(BF16)

    loop(8, column_ones)

    loads[3].wait()

    def order_targets(u):
        for k in range(8):
            rows = tgt[pl.ds(128 * u + 16 * k, 16), :].astype(F32)
            p = rev_const(k, 3)
            ts[u, pl.ds(p, 8, stride=8), :] = rows[0:8]
            ts[u, pl.ds(64 + p, 8, stride=8), :] = rows[8:16]

    loop(8, order_targets)

    loop(15, lambda j: arrived(wbin.at[peer(j, -1)], r1.at[peer(j, -1)], "factor", peer(j, -1)))
    wflat = wbin[...].reshape(128, 128)
    wtb[0:128, :] = wflat
    wtb[128:256, :] = wflat.T

    def spread_b(u):
        for s in range(3):
            for h in range(2):
                rows = pltpu.roll(wtb[64 * h + s : 64 * h + s + 57 : 8, :], lax.rem(128 - u, 128), axis=1)
                for kind in range(2):
                    for p in range(8):
                        k = 64 * kind + 8 * p
                        w1[kind, s, u, 2 * p + h] = jnp.broadcast_to(rows[:, k : k + 1], (8, 128))
        for kind in range(2):
            rows = wtb[pl.ds(128 + 64 * kind + u, 8, stride=8), :]
            for s in range(4):
                for f in range(16):
                    k = 8 * f + 4 + s
                    w2[kind, s, u, f] = jnp.broadcast_to(rows[:, k : k + 1], (8, 128))

    def side_b(w, k):
        u = UP * w + k
        x = [inb[w, pl.ds(64 * UP * h + 8 * k + p, 8, stride=8 * UP), :] for p in range(8) for h in range(2)]
        for s in range(3):
            for i in range(16):
                f1[s, u, i] = x[i]
            x = forward_pairs(x, 2 ** (s + 1), lambda i: w1[0, s, u, i], lambda i: w1[1, s, u, i])
        for i in range(16):
            f2[0, u, pl.ds(64 * (i % 2) + i // 2, 8, stride=8), :] = x[i]
        x = [f2[0, u, tile(f), :] for f in range(16)]
        for s in range(4):
            if s > 0:
                for f in range(16):
                    f2[s, u, tile(f), :] = x[f]
            x = forward_pairs(x, 2**s, lambda f: w2[0, s, u, f], lambda f: w2[1, s, u, f])
        b = []
        for f in range(16):
            place = tile(rev_const(f, 4))
            error = x[f] - ts[u, place, :]
            es[u, place, :] = error
            b.append((2.0 / TOKENS) * error)
        for s in range(3, -1, -1):
            for f in range(16):
                b2[s, u, tile(f), :] = b[f]
            b = backward_pairs(b, 2**s, lambda f: w2[0, s, u, f], lambda f: w2[1, s, u, f])
        for f in range(16):
            b2[4, u, tile(f), :] = b[f]
        b = [b2[4, u, pl.ds(64 * h + p, 8, stride=8), :] for p in range(8) for h in range(2)]
        for s in range(2, -1, -1):
            for i in range(16):
                b1[s, u, i] = b[i]
            b = backward_pairs(b, 2 ** (s + 1), lambda i: w1[0, s, u, i], lambda i: w1[1, s, u, i])
        for i in range(16):
            outb[w, pl.ds(64 * UP * (i % 2) + 8 * k + i // 2, 8, stride=8 * UP), :] = b[i]

    def copy_b(f, w):
        return pltpu.make_async_remote_copy(
            src_ref=outb.at[w, pl.ds(8 * UP * f, 8 * UP)], dst_ref=ina.at[mine, pl.ds(8 * UP * w, 8 * UP)],
            send_sem=s3.at[w, f], recv_sem=r3.at[w, mine], device_id={"factor": f}, device_id_type=MESH,
        )

    def part_b(w):
        loop(UP, lambda k: spread_b(UP * w + k))
        loop(
            15,
            lambda j: arrived(
                inb.at[w, pl.ds(8 * UP * peer(14 - j, -1), 8 * UP)], r2.at[w, peer(14 - j, -1)], "factor", peer(14 - j, -1)
            ),
        )
        loop(UP, lambda k: side_b(w, k))
        loop(15, lambda j: copy_b(peer(j, 1), w).start())
        ina[mine, pl.ds(8 * UP * w, 8 * UP), :] = outb[w, pl.ds(8 * UP * me, 8 * UP), :]

    loop(PARTS, part_b)

    def order_errors(u):
        for k in range(8):
            p = rev_const(k, 3)
            for h in range(2):
                res[pl.ds(128 * u + 16 * k + 8 * h, 8), :] = es[u, pl.ds(64 * h + p, 8, stride=8), :]

    loop(8, order_errors)

    def grads_high(u):
        total = None
        for s in range(4):
            blocks = [
                b2[s, u, tile(f), :] * f2[s, u, tile(f ^ 2**s if kind else f), :] for kind in range(2) for f in range(16)
            ]
            term = lane_sums(blocks, 4 + s)
            total = term if total is None else total + term
        for kind in range(2):
            gz[pl.ds(64 * kind + u, 8, stride=8), :] = choose(tiles_of(total, kind))

    loop(8, grads_high)
    gt[...] = gz[...].T
    partb[...] = jnp.zeros_like(partb)

    def grads_low(u):
        for s in range(3):
            blocks = [
                b1[s, u, 2 * p + h] * f1[s, u, 2 * (p ^ 2**s if kind else p) + h]
                for h in range(2) for kind in range(2) for p in range(8)
            ]
            sums = lane_sums(blocks, u)
            for h in range(2):
                partb[s, h] = partb[s, h] + choose(tiles_of(sums, h))

    loop(8, grads_low)
    for s in range(3):
        for h in range(2):
            gt[64 * h + s : 64 * h + s + 57 : 8, :] = partb[s, h]

    def copy_g(f):
        return pltpu.make_async_remote_copy(
            src_ref=gt.at[pl.ds(8 * f, 8)], dst_ref=gin.at[pl.ds(8 * mine, 8)],
            send_sem=s4.at[f], recv_sem=r4.at[mine], device_id={"factor": f}, device_id_type=MESH,
        )

    loop(15, lambda j: copy_g(peer(j, 1)).start())
    gin[pl.ds(8 * mine, 8), :] = gt[pl.ds(8 * me, 8), :]

    def arrived_a(w):
        loop(
            15,
            lambda j: arrived(
                ina.at[rev4(peer(14 - j, -1)), pl.ds(8 * UP * w, 8 * UP)], r3.at[w, rev4(peer(14 - j, -1))],
                "factor", peer(14 - j, -1),
            ),
        )

    def level_a(s, u0):
        u1 = u0 + 2 ** (6 - s)
        rows = [pl.ds(8 * u0, 8), pl.ds(8 * u1, 8)]
        source = ina if s == 6 else b5.at[6 - s - 1]
        b = [[source[a, r, :] for r in rows] for a in range(16)]
        blocks = [
            b[a][k] * fa[s, a, rows[k ^ kind], :] for k in range(2) for kind in range(2) for a in range(16)
        ]
        sums = lane_sums(blocks, s)
        for k, u in ((0, u0), (1, u1)):
            for kind in range(2):
                term = choose(tiles_of(sums, 2 * k + kind))
                parta[kind, u] = term if s == 6 else parta[kind, u] + term
        for a in range(16):
            for k in range(2):
                b5[6 - s, a, rows[k], :] = (
                    wa[0, s, a, rows[k], :] * b[a][k] + wa[1, s, a, rows[1 - k], :] * b[a][1 - k]
                )

    for w in range(PARTS):
        arrived_a(w)
        if UP == 2:
            level_a(6, 2 * w)
            if w % 2 == 1:
                loop(2, lambda k: level_a(5, 2 * w - 2 + k))
        else:
            loop(UP // 2, lambda k: level_a(6, UP * w + 2 * k))
            loop(UP // 2, lambda k: level_a(5, UP * w + 4 * lax.div(k, 2) + lax.rem(k, 2)))
    loop(4, lambda k: level_a(4, k))

    def last_a(u):
        here = pl.ds(8 * u, 8)
        b = [b5[2, a, here, :] for a in range(16)]
        total = None
        for s in range(3, -1, -1):
            blocks = [b[a] * fa[s, a ^ (kind * 2**s), here, :] for kind in range(2) for a in range(16)]
            term = lane_sums(blocks, s)
            total = term if total is None else total + term
            if s > 0:
                b = backward_pairs(b, 2**s, lambda a: wa[0, s, a, here, :], lambda a: wa[1, s, a, here, :])
        for kind in range(2):
            gpart[pl.ds(128 * kind + u, 8, stride=16), :] = parta[kind, u] + choose(tiles_of(total, kind))

    loop(8, last_a)

    loop(15, lambda j: arrived(gin.at[pl.ds(8 * rev4(peer(j, -1)), 8)], r4.at[rev4(peer(j, -1))], "factor", peer(j, -1)))
    turned = gin[...].T
    for c in range(16):
        gpart[16 * c + 8 : 16 * c + 16, :] = turned[8 * c : 8 * c + 8]

    def copy_r(c):
        return pltpu.make_async_remote_copy(
            src_ref=gpart.at[pl.ds(16 * c, 16)], dst_ref=rs.at[col], send_sem=s5.at[c], recv_sem=r5.at[col],
            device_id={"col": c}, device_id_type=MESH,
        )

    def other(j):
        return lax.rem(col + 1 + j, 16)

    loop(15, lambda j: copy_r(other(j)).start())
    rs[col] = gpart[pl.ds(16 * col, 16), :]
    loop(15, lambda j: arrived(rs.at[other(j)], r5.at[other(j)], "col", other(j)))
    terms = [rs[c] for c in range(16)]
    while len(terms) > 1:
        terms = [terms[i] + terms[i + 1] for i in range(0, len(terms), 2)]
    gs[...] = terms[0]
    row_a = lax.rem(lax.broadcasted_iota(jnp.int32, (128, 128), 0), 16)
    lanes = lax.broadcasted_iota(jnp.int32, (128, 128), 1)
    out_row = lax.broadcasted_iota(jnp.int32, (16, 128), 0)
    out_lane = lax.broadcasted_iota(jnp.int32, (16, 128), 1)
    place = lax.rem(out_lane, 8)
    level_of = [place, 7 + place - jnp.where(place > 3, 1, 0)]
    valid = [place != 7, place != 3]
    own_a = lax.div(lanes, 8) == row_a
    total = jnp.zeros((16, 128), F32)
    for k in range(2):
        wide = jnp.concatenate(
            [jnp.broadcast_to(gs[8 * k + rev_const(t, 3) : 8 * k + rev_const(t, 3) + 1, :], (16, 128)) for t in range(8)], axis=0
        )
        wide = jnp.where(own_a, wide, 0.0)
        pick = jnp.where((level_of[k] == out_row) & valid[k], 1.0, 0.0).astype(BF16)
        for part in thirds(wide):
            total = total + lax.dot_general(
                pick, part.astype(BF16), (((1,), (1,)), ((), ())), preferred_element_type=F32
            )
    kind = lax.div(col, 8)
    here = pl.ds(pl.multiple_of(128 * lax.rem(col, 8), 128), 128)
    weights = jnp.where(kind == 0, dg[:, here], cr[:, here])
    gout[col, 0:14] = weights - step_scale * total[0:14]

    def copy_s(c):
        return pltpu.make_async_remote_copy(
            src_ref=gout.at[col], dst_ref=gout.at[col], send_sem=s6.at[c], recv_sem=r6.at[col],
            device_id={"col": c}, device_id_type=MESH,
        )

    loop(15, lambda j: copy_s(other(j)).start())
    loop(15, lambda j: arrived(gout.at[other(j)], r6.at[other(j)], "col", other(j)))
    for p in range(8):
        nd[:, 128 * p : 128 * p + 128] = gout[p, 0:14]
        nc[:, 128 * p : 128 * p + 128] = gout[8 + p, 0:14]

    def drain(j):
        g = peer(j, 1)
        copy_w(g).wait_send()
        copy_g(g).wait_send()
        for w in range(PARTS):
            copy_x(g, w).wait_send()
            copy_b(g, w).wait_send()
        copy_r(other(j)).wait_send()
        copy_s(other(j)).wait_send()

    loop(15, drain)


def write_out(a0, a1, a2, o0, o1, o2, sem):
    copies = [pltpu.make_async_copy(a, o, sem.at[k]) for k, (a, o) in enumerate([(a2, o2), (a0, o0), (a1, o1)])]
    for copy in copies:
        copy.start()
    for copy in copies:
        copy.wait()


def per_device(activations, targets, diagonal, crossing):
    height, width = activations.shape
    plain = lambda *shape: pltpu.VMEM(shape, F32)
    sems = lambda *shape: pltpu.SemaphoreType.DMA(shape)
    vmem, anywhere = pl.BlockSpec(memory_space=pltpu.VMEM), pl.BlockSpec(memory_space=pl.ANY)
    shapes = (diagonal.shape, crossing.shape, (height, width))
    results = pl.pallas_call(
        kernel,
        out_shape=tuple(pltpu.VMEM(shape, F32) for shape in shapes),
        in_specs=[anywhere] * 4,
        out_specs=(vmem,) * 3,
        scratch_shapes=[
            pltpu.VMEM((1024, 128), BF16), pltpu.VMEM((1024, 128), BF16),
            plain(14, 1024), plain(14, 1024),
            plain(1024, 128), plain(8, 128, 128), plain(8, 128, 128), plain(128, 1024), plain(1024, 128),
            pltpu.VMEM((1024, 128), BF16), pltpu.VMEM((8, 256, 128), BF16), plain(128, 128), plain(16, 8, 128), plain(16, 8, 128),
            plain(256, 128),
            plain(2, 7, 16, 64, 128), plain(2, 3, 8, 16, 8, 128), plain(2, 4, 8, 16, 8, 128),
            plain(7, 16, 64, 128), plain(3, 16, 64, 128),
            plain(3, 8, 16, 8, 128), plain(4, 8, 128, 128), plain(3, 8, 16, 8, 128), plain(5, 8, 128, 128),
            plain(16, 64, 128), plain(PARTS, 128 * UP, 128), plain(PARTS, 128 * UP, 128), plain(16, 64, 128),
            plain(2, 8, 8, 128), plain(3, 2, 8, 128), plain(128, 128), plain(128, 128), plain(128, 128),
            plain(256, 128), plain(16, 16, 128), plain(16, 128), plain(16, 16, 128),
            sems(4),
            sems(16), sems(16), sems(PARTS, 16), sems(PARTS, 16), sems(PARTS, 16), sems(PARTS, 16),
            sems(16), sems(16), sems(16), sems(16), sems(16), sems(16),
        ],
        compiler_params=pltpu.CompilerParams(
            collective_id=0, has_side_effects=True, vmem_limit_bytes=56 * 2**20
        ),
    )(activations, targets, diagonal, crossing)
    return pl.pallas_call(
        write_out,
        out_shape=tuple(jax.ShapeDtypeStruct(shape, F32) for shape in shapes),
        in_specs=[anywhere] * 3,
        out_specs=(anywhere,) * 3,
        scratch_shapes=[sems(3)],
        compiler_params=pltpu.CompilerParams(vmem_limit_bytes=2**20),
    )(*results)


def solution(mesh):
    placed = (P("factor", "col"), P("factor", "col"), P(None, "factor"), P(None, "factor"))
    return jax.shard_map(
        per_device,
        mesh=mesh,
        in_specs=placed,
        out_specs=(P(None, "factor"), P(None, "factor"), P("factor", "col")),
        check_vma=False,
    )
```

```python
import jax
import jax.numpy as jnp
from jax import lax
from jax.experimental import pallas as pl
from jax.experimental.pallas import tpu as pltpu
from jax.sharding import PartitionSpec as P

MESH = pl.DeviceIdType.MESH
F32, BF16 = jnp.float32, jnp.bfloat16
step_scale = 0.03
TOKENS = 2048
PARTS = 4
UP = 8 // PARTS


def bit(value, place):
    return lax.rem(lax.div(value, 2**place), 2)


def rev3(v):
    return bit(v, 0) * 4 + bit(v, 1) * 2 + bit(v, 2)


def rev4(v):
    return bit(v, 0) * 8 + bit(v, 1) * 4 + bit(v, 2) * 2 + bit(v, 3)


def rev_const(v, bits):
    return int(format(v, "0%db" % bits)[::-1], 2)


def slot(s):
    return s + (s >= 3)


def forward_pairs(x, span, diag, cross):
    return [diag(i) * x[i] + cross(i) * x[i ^ span] for i in range(len(x))]


def backward_pairs(b, span, diag, cross):
    carried = [cross(i) * b[i] for i in range(len(b))]
    return [diag(i) * b[i] + carried[i ^ span] for i in range(len(b))]


def loop(count, body, unroll=1):
    def step(j, carry):
        body(j)
        return carry

    lax.fori_loop(0, count, step, 0, unroll=unroll)


def thirds(value):
    high = value.astype(BF16).astype(F32)
    rest = value - high
    middle = rest.astype(BF16).astype(F32)
    return high, middle, rest - middle


def kernel(
    act_hbm, tgt_hbm, dg_hbm, cr_hbm,
    nd, nc, res,
    act, tgt, dg, cr,
    xs, ts, es, wst, wt, ewc, ebc, wz, wmsg, wbin, wtb,
    wa, w1, w2, fa, b5, f1, f2, b1, b2,
    outa, inb, outb, ina, parta, partb, gz, gt, gin, gpart, rs, gs, gout,
    ld, s1, r1, s2, r2, s3, r3, s4, r4, s5, r5, s6, r6,
):
    me = lax.axis_index("factor")
    col = lax.axis_index("col")
    mx, mz = lax.div(me, 8), lax.rem(me, 8)
    mine = rev4(me)

    loads = [
        pltpu.make_async_copy(a, b, ld.at[k])
        for k, (a, b) in enumerate([(act_hbm, act), (dg_hbm, dg), (cr_hbm, cr), (tgt_hbm, tgt)])
    ]
    for copy in loads:
        copy.start()

    barrier = pltpu.get_barrier_semaphore()

    def peer(j, sign):
        dx = 1 - lax.div(j, 8)
        dz = lax.rem(dx * (j + 4) + (1 - dx) * (j - 7), 8)
        return lax.rem(mx + dx, 2) * 8 + lax.rem(mz + sign * dz + 8, 8)

    def greet(j):
        pl.semaphore_signal(barrier, inc=1, device_id={"factor": peer(j, 1)}, device_id_type=MESH)
        pl.semaphore_signal(
            barrier, inc=1, device_id={"col": lax.rem(col + 1 + j, 16)}, device_id_type=MESH
        )

    loop(15, greet)

    lane = lax.broadcasted_iota(jnp.int32, (8, 128), 1)
    lane_low = [lax.rem(lax.div(lane, 2**k), 2) == 0 for k in range(7)]

    def choose(tiles):
        k = 3
        while len(tiles) > 1:
            tiles = [jnp.where(lane_low[k], tiles[i], tiles[i + 1]) for i in range(0, len(tiles), 2)]
            k += 1
        return tiles[0]

    def lane_sums(blocks, n):
        block = jnp.concatenate(blocks, axis=0)
        high = block.astype(BF16)
        low = (block - high.astype(F32)).astype(BF16)
        return jnp.dot(jnp.concatenate([high, low], axis=1), ebc[n], preferred_element_type=F32)

    def tiles_of(block, k):
        return [block[128 * k + 8 * i : 128 * k + 8 * i + 8] for i in range(16)]

    def column_pairs(s):
        rows = lax.broadcasted_iota(jnp.int32, (128, 256), 0)
        kind = lax.div(lax.broadcasted_iota(jnp.int32, (128, 256), 1), 128)
        chosen = (lax.rem(rows, 32) == 16 * kind + s) & (rows < 96)
        ewc[s] = jnp.where(chosen, 1.0, 0.0).astype(BF16)

    loop(7, column_pairs)

    wst[96:128, :] = jnp.zeros((32, 1024), F32)
    loads[0].wait()

    def convert(j):
        here = pl.ds(16 * j, 16)
        xs[here, :] = act[here, :].astype(F32)

    loop(64, convert, 4)
    loads[1].wait()
    loads[2].wait()
    for s in range(14):
        row = 96 + (s if s < 7 else 8 + slot(s - 7))
        wst[row : row + 1, :] = dg[s : s + 1, :]
        wst[16 + row : 17 + row, :] = cr[s : s + 1, :]
    high, middle, rest = thirds(wst[96:128, :])
    wst[0:32, :] = high
    wst[32:64, :] = middle
    wst[64:96, :] = rest
    for k in range(8):
        wt[128 * k : 128 * k + 128, :] = wst[:, 128 * k : 128 * k + 128].T

    def forward_a(u):
        t = rev3(u)
        here = pl.ds(8 * u, 8)
        rows = [wt[pl.ds(16 * t + a, 8, stride=128), :] for a in range(16)]
        columns = jnp.concatenate(rows, axis=0).astype(BF16)
        x = [xs[pl.ds(16 * t + a, 8, stride=128), :] for a in range(16)]
        for s in range(7):
            wide = jnp.dot(columns, ewc[s], preferred_element_type=F32)
            own = [wide[8 * a : 8 * a + 8, 0:128] for a in range(16)]
            beside = [wide[8 * a : 8 * a + 8, 128:256] for a in range(16)]
            for a in range(16):
                wa[0, s, a, here, :] = own[a]
                wa[1, s, a, here, :] = beside[a]
            if s < 4:
                for a in range(16):
                    fa[s, a, here, :] = x[a]
                x = forward_pairs(x, 2**s, lambda a: own[a], lambda a: beside[a])
        for a in range(16):
            fa[4, a, here, :] = x[a]

    loop(8, forward_a, 4)

    def tile(k):
        return slice(8 * k, 8 * k + 8)

    def finish_a(a):
        x = [fa[4, a, tile(u), :] for u in range(8)]
        for s in range(4, 7):
            if s > 4:
                for u in range(8):
                    fa[s, a, tile(u), :] = x[u]
            x = forward_pairs(
                x, 2 ** (6 - s), lambda u: wa[0, s, a, tile(u), :], lambda u: wa[1, s, a, tile(u), :]
            )
        for u in range(8):
            outa[a, tile(u), :] = x[u]

    loop(16, finish_a, 4)

    pl.semaphore_wait(barrier, 30)

    def copy_w(g):
        return pltpu.make_async_remote_copy(
            src_ref=wmsg.at[rev4(g)], dst_ref=wbin.at[me], send_sem=s1.at[g], recv_sem=r1.at[me],
            device_id={"factor": g}, device_id_type=MESH,
        )

    def copy_x(g, w):
        return pltpu.make_async_remote_copy(
            src_ref=outa.at[rev4(g), pl.ds(8 * UP * w, 8 * UP)], dst_ref=inb.at[w, pl.ds(8 * UP * me, 8 * UP)],
            send_sem=s2.at[w, g], recv_sem=r2.at[w, me], device_id={"factor": g}, device_id_type=MESH,
        )

    def arrived(place, sem, axis, source):
        pltpu.make_async_remote_copy(
            src_ref=place, dst_ref=place, send_sem=sem, recv_sem=sem, device_id={axis: source}, device_id_type=MESH
        ).wait_recv()

    loop(15, lambda j: copy_x(peer(j, 1), 0).start())

    def pack_w(u):
        t = rev3(u)
        packed = [jnp.zeros((8, 128), F32) for kind in range(2)]
        for a in range(16):
            rows = wt[pl.ds(16 * t + a, 8, stride=128), :]
            for kind in range(2):
                moved = pltpu.roll(rows, (8 * a - 104 - 16 * kind) % 128, axis=1)
                packed[kind] = jnp.where(lax.div(lane, 8) == a, moved, packed[kind])
        for kind in range(2):
            wz[pl.ds(64 * kind + u, 8, stride=8), :] = packed[kind]

    loop(8, pack_w, 2)
    wmsg[...] = wz[...].T.reshape(16, 8, 128)
    loop(15, lambda j: copy_w(peer(j, 1)).start())
    for w in range(1, PARTS):
        loop(15, lambda j: copy_x(peer(j, 1), w).start())
    wbin[me] = wmsg[mine]
    for w in range(PARTS):
        inb[w, pl.ds(8 * UP * me, 8 * UP), :] = outa[mine, 8 * UP * w : 8 * UP * w + 8 * UP, :]

    def column_ones(n):
        chosen = lax.rem(lax.broadcasted_iota(jnp.int32, (256, 128), 1), 8) == n
        ebc[n] = jnp.where(chosen, 1.0, 0.0).astype(BF16)

    loop(8, column_ones)

    loads[3].wait()

    def order_targets(u):
        for k in range(8):
            rows = tgt[pl.ds(128 * u + 16 * k, 16), :].astype(F32)
            p = rev_const(k, 3)
            ts[u, pl.ds(p, 8, stride=8), :] = rows[0:8]
            ts[u, pl.ds(64 + p, 8, stride=8), :] = rows[8:16]

    loop(8, order_targets)

    loop(15, lambda j: arrived(wbin.at[peer(j, -1)], r1.at[peer(j, -1)], "factor", peer(j, -1)))
    wflat = wbin[...].reshape(128, 128)
    wtb[0:128, :] = wflat
    wtb[128:256, :] = wflat.T

    def spread_b(u):
        for s in range(3):
            for h in range(2):
                rows = pltpu.roll(wtb[64 * h + s : 64 * h + s + 57 : 8, :], lax.rem(128 - u, 128), axis=1)
                for kind in range(2):
                    for p in range(8):
                        k = 64 * kind + 8 * p
                        w1[kind, s, u, 2 * p + h] = jnp.broadcast_to(rows[:, k : k + 1], (8, 128))
        for kind in range(2):
            rows = wtb[pl.ds(128 + 64 * kind + u, 8, stride=8), :]
            for s in range(4):
                for f in range(16):
                    k = 8 * f + 4 + s
                    w2[kind, s, u, f] = jnp.broadcast_to(rows[:, k : k + 1], (8, 128))

    def side_b(w, k):
        u = UP * w + k
        x = [inb[w, pl.ds(64 * UP * h + 8 * k + p, 8, stride=8 * UP), :] for p in range(8) for h in range(2)]
        for s in range(3):
            for i in range(16):
                f1[s, u, i] = x[i]
            x = forward_pairs(x, 2 ** (s + 1), lambda i: w1[0, s, u, i], lambda i: w1[1, s, u, i])
        for i in range(16):
            f2[0, u, pl.ds(64 * (i % 2) + i // 2, 8, stride=8), :] = x[i]
        x = [f2[0, u, tile(f), :] for f in range(16)]
        for s in range(4):
            if s > 0:
                for f in range(16):
                    f2[s, u, tile(f), :] = x[f]
            x = forward_pairs(x, 2**s, lambda f: w2[0, s, u, f], lambda f: w2[1, s, u, f])
        b = []
        for f in range(16):
            place = tile(rev_const(f, 4))
            error = x[f] - ts[u, place, :]
            es[u, place, :] = error
            b.append((2.0 / TOKENS) * error)
        for s in range(3, -1, -1):
            for f in range(16):
                b2[s, u, tile(f), :] = b[f]
            b = backward_pairs(b, 2**s, lambda f: w2[0, s, u, f], lambda f: w2[1, s, u, f])
        for f in range(16):
            b2[4, u, tile(f), :] = b[f]
        b = [b2[4, u, pl.ds(64 * h + p, 8, stride=8), :] for p in range(8) for h in range(2)]
        for s in range(2, -1, -1):
            for i in range(16):
                b1[s, u, i] = b[i]
            b = backward_pairs(b, 2 ** (s + 1), lambda i: w1[0, s, u, i], lambda i: w1[1, s, u, i])
        for i in range(16):
            outb[w, pl.ds(64 * UP * (i % 2) + 8 * k + i // 2, 8, stride=8 * UP), :] = b[i]

    def copy_b(f, w):
        return pltpu.make_async_remote_copy(
            src_ref=outb.at[w, pl.ds(8 * UP * f, 8 * UP)], dst_ref=ina.at[mine, pl.ds(8 * UP * w, 8 * UP)],
            send_sem=s3.at[w, f], recv_sem=r3.at[w, mine], device_id={"factor": f}, device_id_type=MESH,
        )

    def part_b(w):
        loop(UP, lambda k: spread_b(UP * w + k), 2)
        loop(
            15,
            lambda j: arrived(
                inb.at[w, pl.ds(8 * UP * peer(14 - j, -1), 8 * UP)], r2.at[w, peer(14 - j, -1)], "factor", peer(14 - j, -1)
            ),
        )
        loop(UP, lambda k: side_b(w, k), 2)
        loop(15, lambda j: copy_b(peer(j, 1), w).start())
        ina[mine, pl.ds(8 * UP * w, 8 * UP), :] = outb[w, pl.ds(8 * UP * me, 8 * UP), :]

    loop(PARTS, part_b)

    def order_errors(u):
        for k in range(8):
            p = rev_const(k, 3)
            for h in range(2):
                res[pl.ds(128 * u + 16 * k + 8 * h, 8), :] = es[u, pl.ds(64 * h + p, 8, stride=8), :]

    loop(8, order_errors)

    def grads_high(u):
        total = None
        for s in range(4):
            blocks = [
                b2[s, u, tile(f), :] * f2[s, u, tile(f ^ 2**s if kind else f), :] for kind in range(2) for f in range(16)
            ]
            term = lane_sums(blocks, 4 + s)
            total = term if total is None else total + term
        for kind in range(2):
            gz[pl.ds(64 * kind + u, 8, stride=8), :] = choose(tiles_of(total, kind))

    loop(8, grads_high)
    gt[...] = gz[...].T
    partb[...] = jnp.zeros_like(partb)

    def grads_low(u):
        for s in range(3):
            blocks = [
                b1[s, u, 2 * p + h] * f1[s, u, 2 * (p ^ 2**s if kind else p) + h]
                for h in range(2) for kind in range(2) for p in range(8)
            ]
            sums = lane_sums(blocks, u)
            for h in range(2):
                partb[s, h] = partb[s, h] + choose(tiles_of(sums, h))

    loop(8, grads_low)
    for s in range(3):
        for h in range(2):
            gt[64 * h + s : 64 * h + s + 57 : 8, :] = partb[s, h]

    def copy_g(f):
        return pltpu.make_async_remote_copy(
            src_ref=gt.at[pl.ds(8 * f, 8)], dst_ref=gin.at[pl.ds(8 * mine, 8)],
            send_sem=s4.at[f], recv_sem=r4.at[mine], device_id={"factor": f}, device_id_type=MESH,
        )

    loop(15, lambda j: copy_g(peer(j, 1)).start())
    gin[pl.ds(8 * mine, 8), :] = gt[pl.ds(8 * me, 8), :]

    def drain_first(j):
        g = peer(j, 1)
        copy_w(g).wait_send()
        for w in range(PARTS):
            copy_x(g, w).wait_send()

    loop(15, drain_first)

    def arrived_a(w):
        loop(
            15,
            lambda j: arrived(
                ina.at[rev4(peer(14 - j, -1)), pl.ds(8 * UP * w, 8 * UP)], r3.at[w, rev4(peer(14 - j, -1))],
                "factor", peer(14 - j, -1),
            ),
        )

    def level_a(s, u0):
        u1 = u0 + 2 ** (6 - s)
        rows = [pl.ds(8 * u0, 8), pl.ds(8 * u1, 8)]
        source = ina if s == 6 else b5.at[6 - s - 1]
        b = [[source[a, r, :] for r in rows] for a in range(16)]
        blocks = [
            b[a][k] * fa[s, a, rows[k ^ kind], :] for k in range(2) for kind in range(2) for a in range(16)
        ]
        sums = lane_sums(blocks, s)
        for k, u in ((0, u0), (1, u1)):
            for kind in range(2):
                term = choose(tiles_of(sums, 2 * k + kind))
                parta[kind, u] = term if s == 6 else parta[kind, u] + term
        for a in range(16):
            for k in range(2):
                b5[6 - s, a, rows[k], :] = (
                    wa[0, s, a, rows[k], :] * b[a][k] + wa[1, s, a, rows[1 - k], :] * b[a][1 - k]
                )

    for w in range(PARTS):
        arrived_a(w)
        if UP == 2:
            level_a(6, 2 * w)
            if w % 2 == 1:
                loop(2, lambda k: level_a(5, 2 * w - 2 + k), 2)
        else:
            loop(UP // 2, lambda k: level_a(6, UP * w + 2 * k))
            loop(UP // 2, lambda k: level_a(5, UP * w + 4 * lax.div(k, 2) + lax.rem(k, 2)))
    loop(4, lambda k: level_a(4, k), 2)

    def last_a(u):
        here = pl.ds(8 * u, 8)
        b = [b5[2, a, here, :] for a in range(16)]
        total = None
        for s in range(3, -1, -1):
            blocks = [b[a] * fa[s, a ^ (kind * 2**s), here, :] for kind in range(2) for a in range(16)]
            term = lane_sums(blocks, s)
            total = term if total is None else total + term
            if s > 0:
                b = backward_pairs(b, 2**s, lambda a: wa[0, s, a, here, :], lambda a: wa[1, s, a, here, :])
        for kind in range(2):
            gpart[pl.ds(128 * kind + u, 8, stride=16), :] = parta[kind, u] + choose(tiles_of(total, kind))

    loop(8, last_a, 4)

    loop(15, lambda j: arrived(gin.at[pl.ds(8 * rev4(peer(j, -1)), 8)], r4.at[rev4(peer(j, -1))], "factor", peer(j, -1)))
    turned = gin[...].T
    for c in range(16):
        gpart[16 * c + 8 : 16 * c + 16, :] = turned[8 * c : 8 * c + 8]

    def copy_r(c):
        return pltpu.make_async_remote_copy(
            src_ref=gpart.at[pl.ds(16 * c, 16)], dst_ref=rs.at[col], send_sem=s5.at[c], recv_sem=r5.at[col],
            device_id={"col": c}, device_id_type=MESH,
        )

    def other(j):
        return lax.rem(col + 1 + j, 16)

    loop(15, lambda j: copy_r(other(j)).start())
    rs[col] = gpart[pl.ds(16 * col, 16), :]
    def drain_second(j):
        g = peer(j, 1)
        copy_g(g).wait_send()
        for w in range(PARTS):
            copy_b(g, w).wait_send()

    loop(15, drain_second)
    loop(15, lambda j: arrived(rs.at[other(j)], r5.at[other(j)], "col", other(j)))
    terms = [rs[c] for c in range(16)]
    while len(terms) > 1:
        terms = [terms[i] + terms[i + 1] for i in range(0, len(terms), 2)]
    gs[...] = terms[0]
    row_a = lax.rem(lax.broadcasted_iota(jnp.int32, (128, 128), 0), 16)
    lanes = lax.broadcasted_iota(jnp.int32, (128, 128), 1)
    out_row = lax.broadcasted_iota(jnp.int32, (16, 128), 0)
    out_lane = lax.broadcasted_iota(jnp.int32, (16, 128), 1)
    place = lax.rem(out_lane, 8)
    level_of = [place, 7 + place - jnp.where(place > 3, 1, 0)]
    valid = [place != 7, place != 3]
    own_a = lax.div(lanes, 8) == row_a
    total = jnp.zeros((16, 128), F32)
    for k in range(2):
        wide = jnp.concatenate(
            [jnp.broadcast_to(gs[8 * k + rev_const(t, 3) : 8 * k + rev_const(t, 3) + 1, :], (16, 128)) for t in range(8)], axis=0
        )
        wide = jnp.where(own_a, wide, 0.0)
        pick = jnp.where((level_of[k] == out_row) & valid[k], 1.0, 0.0).astype(BF16)
        for part in thirds(wide):
            total = total + lax.dot_general(
                pick, part.astype(BF16), (((1,), (1,)), ((), ())), preferred_element_type=F32
            )
    kind = lax.div(col, 8)
    here = pl.ds(pl.multiple_of(128 * lax.rem(col, 8), 128), 128)
    weights = jnp.where(kind == 0, dg[:, here], cr[:, here])
    gout[col, 0:14] = weights - step_scale * total[0:14]

    def copy_s(c):
        return pltpu.make_async_remote_copy(
            src_ref=gout.at[col], dst_ref=gout.at[col], send_sem=s6.at[c], recv_sem=r6.at[col],
            device_id={"col": c}, device_id_type=MESH,
        )

    loop(15, lambda j: copy_s(other(j)).start())
    loop(15, lambda j: copy_r(other(j)).wait_send())
    loop(15, lambda j: arrived(gout.at[other(j)], r6.at[other(j)], "col", other(j)))
    for p in range(8):
        nd[:, 128 * p : 128 * p + 128] = gout[p, 0:14]
        nc[:, 128 * p : 128 * p + 128] = gout[8 + p, 0:14]

    loop(15, lambda j: copy_s(other(j)).wait_send())


def write_out(a0, a1, a2, o0, o1, o2, sem):
    copies = [pltpu.make_async_copy(a, o, sem.at[k]) for k, (a, o) in enumerate([(a2, o2), (a0, o0), (a1, o1)])]
    for copy in copies:
        copy.start()
    for copy in copies:
        copy.wait()


def per_device(activations, targets, diagonal, crossing):
    height, width = activations.shape
    plain = lambda *shape: pltpu.VMEM(shape, F32)
    sems = lambda *shape: pltpu.SemaphoreType.DMA(shape)
    vmem, anywhere = pl.BlockSpec(memory_space=pltpu.VMEM), pl.BlockSpec(memory_space=pl.ANY)
    shapes = (diagonal.shape, crossing.shape, (height, width))
    results = pl.pallas_call(
        kernel,
        out_shape=tuple(pltpu.VMEM(shape, F32) for shape in shapes),
        in_specs=[anywhere] * 4,
        out_specs=(vmem,) * 3,
        scratch_shapes=[
            pltpu.VMEM((1024, 128), BF16), pltpu.VMEM((1024, 128), BF16),
            plain(14, 1024), plain(14, 1024),
            plain(1024, 128), plain(8, 128, 128), plain(8, 128, 128), plain(128, 1024), plain(1024, 128),
            pltpu.VMEM((7, 128, 256), BF16), pltpu.VMEM((8, 256, 128), BF16), plain(128, 128), plain(16, 8, 128), plain(16, 8, 128),
            plain(256, 128),
            plain(2, 7, 16, 64, 128), plain(2, 3, 8, 16, 8, 128), plain(2, 4, 8, 16, 8, 128),
            plain(7, 16, 64, 128), plain(3, 16, 64, 128),
            plain(3, 8, 16, 8, 128), plain(4, 8, 128, 128), plain(3, 8, 16, 8, 128), plain(5, 8, 128, 128),
            plain(16, 64, 128), plain(PARTS, 128 * UP, 128), plain(PARTS, 128 * UP, 128), plain(16, 64, 128),
            plain(2, 8, 8, 128), plain(3, 2, 8, 128), plain(128, 128), plain(128, 128), plain(128, 128),
            plain(256, 128), plain(16, 16, 128), plain(16, 128), plain(16, 16, 128),
            sems(4),
            sems(16), sems(16), sems(PARTS, 16), sems(PARTS, 16), sems(PARTS, 16), sems(PARTS, 16),
            sems(16), sems(16), sems(16), sems(16), sems(16), sems(16),
        ],
        compiler_params=pltpu.CompilerParams(
            collective_id=0, has_side_effects=True, vmem_limit_bytes=56 * 2**20
        ),
    )(activations, targets, diagonal, crossing)
    return pl.pallas_call(
        write_out,
        out_shape=tuple(jax.ShapeDtypeStruct(shape, F32) for shape in shapes),
        in_specs=[anywhere] * 3,
        out_specs=(anywhere,) * 3,
        scratch_shapes=[sems(3)],
        compiler_params=pltpu.CompilerParams(vmem_limit_bytes=2**20),
    )(*results)


def solution(mesh):
    placed = (P("factor", "col"), P("factor", "col"), P(None, "factor"), P(None, "factor"))
    return jax.shard_map(
        per_device,
        mesh=mesh,
        in_specs=placed,
        out_specs=(P(None, "factor"), P(None, "factor"), P("factor", "col")),
        check_vma=False,
    )
```

```python
import jax
import jax.numpy as jnp
from jax import lax
from jax.experimental import pallas as pl
from jax.experimental.pallas import tpu as pltpu
from jax.sharding import PartitionSpec as P

MESH = pl.DeviceIdType.MESH
F32, BF16 = jnp.float32, jnp.bfloat16
step_scale = 0.03
TOKENS = 2048
PARTS = 4
UP = 8 // PARTS


def bit(value, place):
    return lax.rem(lax.div(value, 2**place), 2)


def rev3(v):
    return bit(v, 0) * 4 + bit(v, 1) * 2 + bit(v, 2)


def rev4(v):
    return bit(v, 0) * 8 + bit(v, 1) * 4 + bit(v, 2) * 2 + bit(v, 3)


def rev_const(v, bits):
    return int(format(v, "0%db" % bits)[::-1], 2)


def slot(s):
    return s + (s >= 3)


def forward_pairs(x, span, diag, cross):
    return [diag(i) * x[i] + cross(i) * x[i ^ span] for i in range(len(x))]


def backward_pairs(b, span, diag, cross):
    carried = [cross(i) * b[i] for i in range(len(b))]
    return [diag(i) * b[i] + carried[i ^ span] for i in range(len(b))]


def loop(count, body, unroll=1):
    def step(j, carry):
        body(j)
        return carry

    lax.fori_loop(0, count, step, 0, unroll=unroll)


def thirds(value):
    high = value.astype(BF16).astype(F32)
    rest = value - high
    middle = rest.astype(BF16).astype(F32)
    return high, middle, rest - middle


def kernel(
    act_hbm, tgt_hbm, dg_hbm, cr_hbm,
    nd, nc, res,
    act, tgt, dg, cr,
    xs, ts, es, wst, wt, ewc, ebc, wz, wmsg, wbin, wtb,
    wa, w1, w2, fa, b5, f1, f2, b1, b2,
    outa, inb, outb, ina, parta, partb, gz, gt, gin, gpart, rs, gs, gout,
    ld, s1, r1, s2, r2, s3, r3, s4, r4, s5, r5, s6, r6,
):
    me = lax.axis_index("factor")
    col = lax.axis_index("col")
    mx, mz = lax.div(me, 8), lax.rem(me, 8)
    mine = rev4(me)

    loads = [
        pltpu.make_async_copy(a, b, ld.at[k])
        for k, (a, b) in enumerate([(act_hbm, act), (dg_hbm, dg), (cr_hbm, cr), (tgt_hbm, tgt)])
    ]
    for copy in loads:
        copy.start()

    barrier = pltpu.get_barrier_semaphore()

    def peer(j, sign):
        dx = 1 - lax.div(j, 8)
        dz = lax.rem(dx * (j + 4) + (1 - dx) * (j - 7), 8)
        return lax.rem(mx + dx, 2) * 8 + lax.rem(mz + sign * dz + 8, 8)

    def greet(j):
        pl.semaphore_signal(barrier, inc=1, device_id={"factor": peer(j, 1)}, device_id_type=MESH)
        pl.semaphore_signal(
            barrier, inc=1, device_id={"col": lax.rem(col + 1 + j, 16)}, device_id_type=MESH
        )

    loop(15, greet)

    lane = lax.broadcasted_iota(jnp.int32, (8, 128), 1)
    lane_low = [lax.rem(lax.div(lane, 2**k), 2) == 0 for k in range(7)]

    def choose(tiles):
        k = 3
        while len(tiles) > 1:
            tiles = [jnp.where(lane_low[k], tiles[i], tiles[i + 1]) for i in range(0, len(tiles), 2)]
            k += 1
        return tiles[0]

    def lane_sums(blocks, n):
        block = jnp.concatenate(blocks, axis=0)
        high = block.astype(BF16)
        low = (block - high.astype(F32)).astype(BF16)
        return jnp.dot(jnp.concatenate([high, low], axis=1), ebc[n], preferred_element_type=F32)

    def tiles_of(block, k):
        return [block[128 * k + 8 * i : 128 * k + 8 * i + 8] for i in range(16)]

    def column_pairs(s):
        rows = lax.broadcasted_iota(jnp.int32, (128, 256), 0)
        kind = lax.div(lax.broadcasted_iota(jnp.int32, (128, 256), 1), 128)
        chosen = (lax.rem(rows, 32) == 16 * kind + s) & (rows < 96)
        ewc[s] = jnp.where(chosen, 1.0, 0.0).astype(BF16)

    loop(7, column_pairs)

    wst[96:128, :] = jnp.zeros((32, 1024), F32)
    loads[0].wait()

    def convert(j):
        here = pl.ds(16 * j, 16)
        xs[here, :] = act[here, :].astype(F32)

    loop(64, convert, 4)
    loads[1].wait()
    loads[2].wait()
    for s in range(14):
        row = 96 + (s if s < 7 else 8 + slot(s - 7))
        wst[row : row + 1, :] = dg[s : s + 1, :]
        wst[16 + row : 17 + row, :] = cr[s : s + 1, :]
    high, middle, rest = thirds(wst[96:128, :])
    wst[0:32, :] = high
    wst[32:64, :] = middle
    wst[64:96, :] = rest
    for k in range(8):
        wt[128 * k : 128 * k + 128, :] = wst[:, 128 * k : 128 * k + 128].T

    def forward_a(u):
        t = rev3(u)
        here = pl.ds(8 * u, 8)
        rows = [wt[pl.ds(16 * t + a, 8, stride=128), :] for a in range(16)]
        columns = jnp.concatenate(rows, axis=0).astype(BF16)
        x = [xs[pl.ds(16 * t + a, 8, stride=128), :] for a in range(16)]
        for s in range(7):
            wide = jnp.dot(columns, ewc[s], preferred_element_type=F32)
            own = [wide[8 * a : 8 * a + 8, 0:128] for a in range(16)]
            beside = [wide[8 * a : 8 * a + 8, 128:256] for a in range(16)]
            for a in range(16):
                wa[0, s, a, here, :] = own[a]
                wa[1, s, a, here, :] = beside[a]
            if s < 4:
                for a in range(16):
                    fa[s, a, here, :] = x[a]
                x = forward_pairs(x, 2**s, lambda a: own[a], lambda a: beside[a])
        for a in range(16):
            fa[4, a, here, :] = x[a]

    loop(8, forward_a, 8)

    def tile(k):
        return slice(8 * k, 8 * k + 8)

    def finish_a(a):
        x = [fa[4, a, tile(u), :] for u in range(8)]
        for s in range(4, 7):
            if s > 4:
                for u in range(8):
                    fa[s, a, tile(u), :] = x[u]
            x = forward_pairs(
                x, 2 ** (6 - s), lambda u: wa[0, s, a, tile(u), :], lambda u: wa[1, s, a, tile(u), :]
            )
        for u in range(8):
            outa[a, tile(u), :] = x[u]

    loop(16, finish_a, 8)

    pl.semaphore_wait(barrier, 30)

    def copy_w(g):
        return pltpu.make_async_remote_copy(
            src_ref=wmsg.at[rev4(g)], dst_ref=wbin.at[me], send_sem=s1.at[g], recv_sem=r1.at[me],
            device_id={"factor": g}, device_id_type=MESH,
        )

    def copy_x(g, w):
        return pltpu.make_async_remote_copy(
            src_ref=outa.at[rev4(g), pl.ds(8 * UP * w, 8 * UP)], dst_ref=inb.at[w, pl.ds(8 * UP * me, 8 * UP)],
            send_sem=s2.at[w, g], recv_sem=r2.at[w, me], device_id={"factor": g}, device_id_type=MESH,
        )

    def arrived(place, sem, axis, source):
        pltpu.make_async_remote_copy(
            src_ref=place, dst_ref=place, send_sem=sem, recv_sem=sem, device_id={axis: source}, device_id_type=MESH
        ).wait_recv()

    loop(15, lambda j: copy_x(peer(j, 1), 0).start())

    def pack_w(u):
        t = rev3(u)
        packed = [jnp.zeros((8, 128), F32) for kind in range(2)]
        for a in range(16):
            rows = wt[pl.ds(16 * t + a, 8, stride=128), :]
            for kind in range(2):
                moved = pltpu.roll(rows, (8 * a - 104 - 16 * kind) % 128, axis=1)
                packed[kind] = jnp.where(lax.div(lane, 8) == a, moved, packed[kind])
        for kind in range(2):
            wz[pl.ds(64 * kind + u, 8, stride=8), :] = packed[kind]

    loop(8, pack_w, 4)
    wmsg[...] = wz[...].T.reshape(16, 8, 128)
    loop(15, lambda j: copy_w(peer(j, 1)).start())
    for w in range(1, PARTS):
        loop(15, lambda j: copy_x(peer(j, 1), w).start())
    wbin[me] = wmsg[mine]
    for w in range(PARTS):
        inb[w, pl.ds(8 * UP * me, 8 * UP), :] = outa[mine, 8 * UP * w : 8 * UP * w + 8 * UP, :]

    def column_ones(n):
        chosen = lax.rem(lax.broadcasted_iota(jnp.int32, (256, 128), 1), 8) == n
        ebc[n] = jnp.where(chosen, 1.0, 0.0).astype(BF16)

    loop(8, column_ones)

    loads[3].wait()

    def order_targets(u):
        for k in range(8):
            rows = tgt[pl.ds(128 * u + 16 * k, 16), :].astype(F32)
            p = rev_const(k, 3)
            ts[u, pl.ds(p, 8, stride=8), :] = rows[0:8]
            ts[u, pl.ds(64 + p, 8, stride=8), :] = rows[8:16]

    loop(8, order_targets)

    loop(15, lambda j: arrived(wbin.at[peer(j, -1)], r1.at[peer(j, -1)], "factor", peer(j, -1)))
    wflat = wbin[...].reshape(128, 128)
    wtb[0:128, :] = wflat
    wtb[128:256, :] = wflat.T

    def spread_b(u):
        for s in range(3):
            for h in range(2):
                rows = pltpu.roll(wtb[64 * h + s : 64 * h + s + 57 : 8, :], lax.rem(128 - u, 128), axis=1)
                for kind in range(2):
                    for p in range(8):
                        k = 64 * kind + 8 * p
                        w1[kind, s, u, 2 * p + h] = jnp.broadcast_to(rows[:, k : k + 1], (8, 128))
        for kind in range(2):
            rows = wtb[pl.ds(128 + 64 * kind + u, 8, stride=8), :]
            for s in range(4):
                for f in range(16):
                    k = 8 * f + 4 + s
                    w2[kind, s, u, f] = jnp.broadcast_to(rows[:, k : k + 1], (8, 128))

    def side_b(w, k):
        u = UP * w + k
        x = [inb[w, pl.ds(64 * UP * h + 8 * k + p, 8, stride=8 * UP), :] for p in range(8) for h in range(2)]
        for s in range(3):
            for i in range(16):
                f1[s, u, i] = x[i]
            x = forward_pairs(x, 2 ** (s + 1), lambda i: w1[0, s, u, i], lambda i: w1[1, s, u, i])
        for i in range(16):
            f2[0, u, pl.ds(64 * (i % 2) + i // 2, 8, stride=8), :] = x[i]
        x = [f2[0, u, tile(f), :] for f in range(16)]
        for s in range(4):
            if s > 0:
                for f in range(16):
                    f2[s, u, tile(f), :] = x[f]
            x = forward_pairs(x, 2**s, lambda f: w2[0, s, u, f], lambda f: w2[1, s, u, f])
        b = []
        for f in range(16):
            place = tile(rev_const(f, 4))
            error = x[f] - ts[u, place, :]
            es[u, place, :] = error
            b.append((2.0 / TOKENS) * error)
        for s in range(3, -1, -1):
            for f in range(16):
                b2[s, u, tile(f), :] = b[f]
            b = backward_pairs(b, 2**s, lambda f: w2[0, s, u, f], lambda f: w2[1, s, u, f])
        for f in range(16):
            b2[4, u, tile(f), :] = b[f]
        b = [b2[4, u, pl.ds(64 * h + p, 8, stride=8), :] for p in range(8) for h in range(2)]
        for s in range(2, -1, -1):
            for i in range(16):
                b1[s, u, i] = b[i]
            b = backward_pairs(b, 2 ** (s + 1), lambda i: w1[0, s, u, i], lambda i: w1[1, s, u, i])
        for i in range(16):
            outb[w, pl.ds(64 * UP * (i % 2) + 8 * k + i // 2, 8, stride=8 * UP), :] = b[i]

    def copy_b(f, w):
        return pltpu.make_async_remote_copy(
            src_ref=outb.at[w, pl.ds(8 * UP * f, 8 * UP)], dst_ref=ina.at[mine, pl.ds(8 * UP * w, 8 * UP)],
            send_sem=s3.at[w, f], recv_sem=r3.at[w, mine], device_id={"factor": f}, device_id_type=MESH,
        )

    def part_b(w):
        loop(UP, lambda k: spread_b(UP * w + k), 2)
        loop(
            15,
            lambda j: arrived(
                inb.at[w, pl.ds(8 * UP * peer(14 - j, -1), 8 * UP)], r2.at[w, peer(14 - j, -1)], "factor", peer(14 - j, -1)
            ),
        )
        loop(UP, lambda k: side_b(w, k), 2)
        loop(15, lambda j: copy_b(peer(j, 1), w).start())
        ina[mine, pl.ds(8 * UP * w, 8 * UP), :] = outb[w, pl.ds(8 * UP * me, 8 * UP), :]

    loop(PARTS, part_b)

    def order_errors(u):
        for k in range(8):
            p = rev_const(k, 3)
            for h in range(2):
                res[pl.ds(128 * u + 16 * k + 8 * h, 8), :] = es[u, pl.ds(64 * h + p, 8, stride=8), :]

    loop(8, order_errors)

    def grads_high(u):
        total = None
        for s in range(4):
            blocks = [
                b2[s, u, tile(f), :] * f2[s, u, tile(f ^ 2**s if kind else f), :] for kind in range(2) for f in range(16)
            ]
            term = lane_sums(blocks, 4 + s)
            total = term if total is None else total + term
        for kind in range(2):
            gz[pl.ds(64 * kind + u, 8, stride=8), :] = choose(tiles_of(total, kind))

    loop(8, grads_high)
    gt[...] = gz[...].T
    partb[...] = jnp.zeros_like(partb)

    def grads_low(u):
        for s in range(3):
            blocks = [
                b1[s, u, 2 * p + h] * f1[s, u, 2 * (p ^ 2**s if kind else p) + h]
                for h in range(2) for kind in range(2) for p in range(8)
            ]
            sums = lane_sums(blocks, u)
            for h in range(2):
                partb[s, h] = partb[s, h] + choose(tiles_of(sums, h))

    loop(8, grads_low)
    for s in range(3):
        for h in range(2):
            gt[64 * h + s : 64 * h + s + 57 : 8, :] = partb[s, h]

    def copy_g(f):
        return pltpu.make_async_remote_copy(
            src_ref=gt.at[pl.ds(8 * f, 8)], dst_ref=gin.at[pl.ds(8 * mine, 8)],
            send_sem=s4.at[f], recv_sem=r4.at[mine], device_id={"factor": f}, device_id_type=MESH,
        )

    loop(15, lambda j: copy_g(peer(j, 1)).start())
    gin[pl.ds(8 * mine, 8), :] = gt[pl.ds(8 * me, 8), :]

    def drain_first(j):
        g = peer(j, 1)
        copy_w(g).wait_send()
        for w in range(PARTS):
            copy_x(g, w).wait_send()

    loop(15, drain_first)

    def arrived_a(w):
        loop(
            15,
            lambda j: arrived(
                ina.at[rev4(peer(14 - j, -1)), pl.ds(8 * UP * w, 8 * UP)], r3.at[w, rev4(peer(14 - j, -1))],
                "factor", peer(14 - j, -1),
            ),
        )

    def level_a(s, u0):
        u1 = u0 + 2 ** (6 - s)
        rows = [pl.ds(8 * u0, 8), pl.ds(8 * u1, 8)]
        source = ina if s == 6 else b5.at[6 - s - 1]
        b = [[source[a, r, :] for r in rows] for a in range(16)]
        blocks = [
            b[a][k] * fa[s, a, rows[k ^ kind], :] for k in range(2) for kind in range(2) for a in range(16)
        ]
        sums = lane_sums(blocks, s)
        for k, u in ((0, u0), (1, u1)):
            for kind in range(2):
                term = choose(tiles_of(sums, 2 * k + kind))
                parta[kind, u] = term if s == 6 else parta[kind, u] + term
        for a in range(16):
            for k in range(2):
                b5[6 - s, a, rows[k], :] = (
                    wa[0, s, a, rows[k], :] * b[a][k] + wa[1, s, a, rows[1 - k], :] * b[a][1 - k]
                )

    for w in range(PARTS):
        arrived_a(w)
        if UP == 2:
            level_a(6, 2 * w)
            if w % 2 == 1:
                loop(2, lambda k: level_a(5, 2 * w - 2 + k), 2)
        else:
            loop(UP // 2, lambda k: level_a(6, UP * w + 2 * k))
            loop(UP // 2, lambda k: level_a(5, UP * w + 4 * lax.div(k, 2) + lax.rem(k, 2)))
    loop(4, lambda k: level_a(4, k), 4)

    def last_a(u):
        here = pl.ds(8 * u, 8)
        b = [b5[2, a, here, :] for a in range(16)]
        total = None
        for s in range(3, -1, -1):
            blocks = [b[a] * fa[s, a ^ (kind * 2**s), here, :] for kind in range(2) for a in range(16)]
            term = lane_sums(blocks, s)
            total = term if total is None else total + term
            if s > 0:
                b = backward_pairs(b, 2**s, lambda a: wa[0, s, a, here, :], lambda a: wa[1, s, a, here, :])
        for kind in range(2):
            gpart[pl.ds(128 * kind + u, 8, stride=16), :] = parta[kind, u] + choose(tiles_of(total, kind))

    loop(8, last_a, 8)

    loop(15, lambda j: arrived(gin.at[pl.ds(8 * rev4(peer(j, -1)), 8)], r4.at[rev4(peer(j, -1))], "factor", peer(j, -1)))
    turned = gin[...].T
    for c in range(16):
        gpart[16 * c + 8 : 16 * c + 16, :] = turned[8 * c : 8 * c + 8]

    def copy_r(c):
        return pltpu.make_async_remote_copy(
            src_ref=gpart.at[pl.ds(16 * c, 16)], dst_ref=rs.at[col], send_sem=s5.at[c], recv_sem=r5.at[col],
            device_id={"col": c}, device_id_type=MESH,
        )

    def other(j):
        return lax.rem(col + 1 + j, 16)

    loop(15, lambda j: copy_r(other(j)).start())
    rs[col] = gpart[pl.ds(16 * col, 16), :]
    def drain_second(j):
        g = peer(j, 1)
        copy_g(g).wait_send()
        for w in range(PARTS):
            copy_b(g, w).wait_send()

    loop(15, drain_second)
    loop(15, lambda j: arrived(rs.at[other(j)], r5.at[other(j)], "col", other(j)))
    terms = [rs[c] for c in range(16)]
    while len(terms) > 1:
        terms = [terms[i] + terms[i + 1] for i in range(0, len(terms), 2)]
    gs[...] = terms[0]
    row_a = lax.rem(lax.broadcasted_iota(jnp.int32, (128, 128), 0), 16)
    lanes = lax.broadcasted_iota(jnp.int32, (128, 128), 1)
    out_row = lax.broadcasted_iota(jnp.int32, (16, 128), 0)
    out_lane = lax.broadcasted_iota(jnp.int32, (16, 128), 1)
    place = lax.rem(out_lane, 8)
    level_of = [place, 7 + place - jnp.where(place > 3, 1, 0)]
    valid = [place != 7, place != 3]
    own_a = lax.div(lanes, 8) == row_a
    total = jnp.zeros((16, 128), F32)
    for k in range(2):
        wide = jnp.concatenate(
            [jnp.broadcast_to(gs[8 * k + rev_const(t, 3) : 8 * k + rev_const(t, 3) + 1, :], (16, 128)) for t in range(8)], axis=0
        )
        wide = jnp.where(own_a, wide, 0.0)
        pick = jnp.where((level_of[k] == out_row) & valid[k], 1.0, 0.0).astype(BF16)
        for part in thirds(wide):
            total = total + lax.dot_general(
                pick, part.astype(BF16), (((1,), (1,)), ((), ())), preferred_element_type=F32
            )
    kind = lax.div(col, 8)
    here = pl.ds(pl.multiple_of(128 * lax.rem(col, 8), 128), 128)
    weights = jnp.where(kind == 0, dg[:, here], cr[:, here])
    gout[col, 0:14] = weights - step_scale * total[0:14]

    def copy_s(c):
        return pltpu.make_async_remote_copy(
            src_ref=gout.at[col], dst_ref=gout.at[col], send_sem=s6.at[c], recv_sem=r6.at[col],
            device_id={"col": c}, device_id_type=MESH,
        )

    loop(15, lambda j: copy_s(other(j)).start())
    loop(15, lambda j: copy_r(other(j)).wait_send())
    loop(15, lambda j: arrived(gout.at[other(j)], r6.at[other(j)], "col", other(j)))
    for p in range(8):
        nd[:, 128 * p : 128 * p + 128] = gout[p, 0:14]
        nc[:, 128 * p : 128 * p + 128] = gout[8 + p, 0:14]

    loop(15, lambda j: copy_s(other(j)).wait_send())


def write_out(a0, a1, a2, o0, o1, o2, sem):
    copies = [pltpu.make_async_copy(a, o, sem.at[k]) for k, (a, o) in enumerate([(a2, o2), (a0, o0), (a1, o1)])]
    for copy in copies:
        copy.start()
    for copy in copies:
        copy.wait()


def per_device(activations, targets, diagonal, crossing):
    height, width = activations.shape
    plain = lambda *shape: pltpu.VMEM(shape, F32)
    sems = lambda *shape: pltpu.SemaphoreType.DMA(shape)
    vmem, anywhere = pl.BlockSpec(memory_space=pltpu.VMEM), pl.BlockSpec(memory_space=pl.ANY)
    shapes = (diagonal.shape, crossing.shape, (height, width))
    results = pl.pallas_call(
        kernel,
        out_shape=tuple(pltpu.VMEM(shape, F32) for shape in shapes),
        in_specs=[anywhere] * 4,
        out_specs=(vmem,) * 3,
        scratch_shapes=[
            pltpu.VMEM((1024, 128), BF16), pltpu.VMEM((1024, 128), BF16),
            plain(14, 1024), plain(14, 1024),
            plain(1024, 128), plain(8, 128, 128), plain(8, 128, 128), plain(128, 1024), plain(1024, 128),
            pltpu.VMEM((7, 128, 256), BF16), pltpu.VMEM((8, 256, 128), BF16), plain(128, 128), plain(16, 8, 128), plain(16, 8, 128),
            plain(256, 128),
            plain(2, 7, 16, 64, 128), plain(2, 3, 8, 16, 8, 128), plain(2, 4, 8, 16, 8, 128),
            plain(7, 16, 64, 128), plain(3, 16, 64, 128),
            plain(3, 8, 16, 8, 128), plain(4, 8, 128, 128), plain(3, 8, 16, 8, 128), plain(5, 8, 128, 128),
            plain(16, 64, 128), plain(PARTS, 128 * UP, 128), plain(PARTS, 128 * UP, 128), plain(16, 64, 128),
            plain(2, 8, 8, 128), plain(3, 2, 8, 128), plain(128, 128), plain(128, 128), plain(128, 128),
            plain(256, 128), plain(16, 16, 128), plain(16, 128), plain(16, 16, 128),
            sems(4),
            sems(16), sems(16), sems(PARTS, 16), sems(PARTS, 16), sems(PARTS, 16), sems(PARTS, 16),
            sems(16), sems(16), sems(16), sems(16), sems(16), sems(16),
        ],
        compiler_params=pltpu.CompilerParams(
            collective_id=0, has_side_effects=True, vmem_limit_bytes=56 * 2**20
        ),
    )(activations, targets, diagonal, crossing)
    return pl.pallas_call(
        write_out,
        out_shape=tuple(jax.ShapeDtypeStruct(shape, F32) for shape in shapes),
        in_specs=[anywhere] * 3,
        out_specs=(anywhere,) * 3,
        scratch_shapes=[sems(3)],
        compiler_params=pltpu.CompilerParams(vmem_limit_bytes=2**20),
    )(*results)


def solution(mesh):
    placed = (P("factor", "col"), P("factor", "col"), P(None, "factor"), P(None, "factor"))
    return jax.shard_map(
        per_device,
        mesh=mesh,
        in_specs=placed,
        out_specs=(P(None, "factor"), P(None, "factor"), P("factor", "col")),
        check_vma=False,
    )
```

```python
import jax
import jax.numpy as jnp
from jax import lax
from jax.experimental import pallas as pl
from jax.experimental.pallas import tpu as pltpu
from jax.sharding import PartitionSpec as P

MESH = pl.DeviceIdType.MESH
F32, BF16 = jnp.float32, jnp.bfloat16
step_scale = 0.03
TOKENS = 2048
PARTS = 4
UP = 8 // PARTS


def bit(value, place):
    return lax.rem(lax.div(value, 2**place), 2)


def rev3(v):
    return bit(v, 0) * 4 + bit(v, 1) * 2 + bit(v, 2)


def rev4(v):
    return bit(v, 0) * 8 + bit(v, 1) * 4 + bit(v, 2) * 2 + bit(v, 3)


def rev_const(v, bits):
    return int(format(v, "0%db" % bits)[::-1], 2)


def slot(s):
    return s + (s >= 3)


def forward_pairs(x, span, diag, cross):
    return [diag(i) * x[i] + cross(i) * x[i ^ span] for i in range(len(x))]


def backward_pairs(b, span, diag, cross):
    carried = [cross(i) * b[i] for i in range(len(b))]
    return [diag(i) * b[i] + carried[i ^ span] for i in range(len(b))]


def loop(count, body, unroll=1):
    def step(j, carry):
        body(j)
        return carry

    lax.fori_loop(0, count, step, 0, unroll=unroll)


def thirds(value):
    high = value.astype(BF16).astype(F32)
    rest = value - high
    middle = rest.astype(BF16).astype(F32)
    return high, middle, rest - middle


def kernel(
    act_hbm, tgt_hbm, dg_hbm, cr_hbm,
    nd, nc, res,
    act, tgt, dg, cr,
    xs, ts, es, wst, wt, ewc, ebc, wz, wmsg, wbin, wtb,
    wa, w1, w2, fa, b5, f1, f2, b1, b2,
    outa, inb, outb, ina, parta, partb, gz, gt, gin, gpart, rs, gs, gout,
    ld, s1, r1, s2, r2, s3, r3, s4, r4, s5, r5, s6, r6,
):
    me = lax.axis_index("factor")
    col = lax.axis_index("col")
    mx, mz = lax.div(me, 8), lax.rem(me, 8)
    mine = rev4(me)

    loads = [
        pltpu.make_async_copy(a, b, ld.at[k])
        for k, (a, b) in enumerate([(act_hbm, act), (dg_hbm, dg), (cr_hbm, cr), (tgt_hbm, tgt)])
    ]
    for copy in loads:
        copy.start()

    barrier = pltpu.get_barrier_semaphore()

    def peer(j, sign):
        dx = 1 - lax.div(j, 8)
        dz = lax.rem(dx * (j + 4) + (1 - dx) * (j - 7), 8)
        return lax.rem(mx + dx, 2) * 8 + lax.rem(mz + sign * dz + 8, 8)

    def greet(j):
        pl.semaphore_signal(barrier, inc=1, device_id={"factor": peer(j, 1)}, device_id_type=MESH)
        pl.semaphore_signal(
            barrier, inc=1, device_id={"col": lax.rem(col + 1 + j, 16)}, device_id_type=MESH
        )

    loop(15, greet)

    lane = lax.broadcasted_iota(jnp.int32, (8, 128), 1)
    lane_low = [lax.rem(lax.div(lane, 2**k), 2) == 0 for k in range(7)]

    def choose(tiles):
        k = 3
        while len(tiles) > 1:
            tiles = [jnp.where(lane_low[k], tiles[i], tiles[i + 1]) for i in range(0, len(tiles), 2)]
            k += 1
        return tiles[0]

    def lane_sums(blocks, n):
        block = jnp.concatenate(blocks, axis=0)
        high = block.astype(BF16)
        low = (block - high.astype(F32)).astype(BF16)
        return jnp.dot(jnp.concatenate([high, low], axis=1), ebc[n], preferred_element_type=F32)

    def tiles_of(block, k):
        return [block[128 * k + 8 * i : 128 * k + 8 * i + 8] for i in range(16)]

    def column_pairs(s):
        rows = lax.broadcasted_iota(jnp.int32, (128, 256), 0)
        kind = lax.div(lax.broadcasted_iota(jnp.int32, (128, 256), 1), 128)
        chosen = (lax.rem(rows, 32) == 16 * kind + s) & (rows < 96)
        ewc[s] = jnp.where(chosen, 1.0, 0.0).astype(BF16)

    loop(7, column_pairs)

    wst[96:128, :] = jnp.zeros((32, 1024), F32)
    loads[0].wait()

    def convert(j):
        here = pl.ds(16 * j, 16)
        xs[here, :] = act[here, :].astype(F32)

    loop(64, convert, 4)
    loads[1].wait()
    loads[2].wait()
    for s in range(14):
        row = 96 + (s if s < 7 else 8 + slot(s - 7))
        wst[row : row + 1, :] = dg[s : s + 1, :]
        wst[16 + row : 17 + row, :] = cr[s : s + 1, :]
    high, middle, rest = thirds(wst[96:128, :])
    wst[0:32, :] = high
    wst[32:64, :] = middle
    wst[64:96, :] = rest
    for k in range(8):
        wt[128 * k : 128 * k + 128, :] = wst[:, 128 * k : 128 * k + 128].T

    def forward_a(u):
        t = rev3(u)
        here = pl.ds(8 * u, 8)
        rows = [wt[pl.ds(16 * t + a, 8, stride=128), :] for a in range(16)]
        columns = jnp.concatenate(rows, axis=0).astype(BF16)
        x = [xs[pl.ds(16 * t + a, 8, stride=128), :] for a in range(16)]
        for s in range(7):
            wide = jnp.dot(columns, ewc[s], preferred_element_type=F32)
            own = [wide[8 * a : 8 * a + 8, 0:128] for a in range(16)]
            beside = [wide[8 * a : 8 * a + 8, 128:256] for a in range(16)]
            for a in range(16):
                wa[0, s, a, here, :] = own[a]
                wa[1, s, a, here, :] = beside[a]
            if s < 4:
                for a in range(16):
                    fa[s, a, here, :] = x[a]
                x = forward_pairs(x, 2**s, lambda a: own[a], lambda a: beside[a])
        for a in range(16):
            fa[4, a, here, :] = x[a]

    loop(8, forward_a, 8)

    def tile(k):
        return slice(8 * k, 8 * k + 8)

    def finish_a(a):
        x = [fa[4, a, tile(u), :] for u in range(8)]
        for s in range(4, 7):
            if s > 4:
                for u in range(8):
                    fa[s, a, tile(u), :] = x[u]
            x = forward_pairs(
                x, 2 ** (6 - s), lambda u: wa[0, s, a, tile(u), :], lambda u: wa[1, s, a, tile(u), :]
            )
        for u in range(8):
            outa[a, tile(u), :] = x[u]

    loop(16, finish_a, 8)

    def pack_w(u):
        t = rev3(u)
        packed = [jnp.zeros((8, 128), F32) for kind in range(2)]
        for a in range(16):
            rows = wt[pl.ds(16 * t + a, 8, stride=128), :]
            for kind in range(2):
                moved = pltpu.roll(rows, (8 * a - 104 - 16 * kind) % 128, axis=1)
                packed[kind] = jnp.where(lax.div(lane, 8) == a, moved, packed[kind])
        for kind in range(2):
            wz[pl.ds(64 * kind + u, 8, stride=8), :] = packed[kind]

    loop(8, pack_w, 4)
    wmsg[...] = wz[...].T.reshape(16, 8, 128)
    pl.semaphore_wait(barrier, 30)

    def copy_w(g):
        return pltpu.make_async_remote_copy(
            src_ref=wmsg.at[rev4(g)], dst_ref=wbin.at[me], send_sem=s1.at[g], recv_sem=r1.at[me],
            device_id={"factor": g}, device_id_type=MESH,
        )

    def copy_x(g, w):
        return pltpu.make_async_remote_copy(
            src_ref=outa.at[rev4(g), pl.ds(8 * UP * w, 8 * UP)], dst_ref=inb.at[w, pl.ds(8 * UP * me, 8 * UP)],
            send_sem=s2.at[w, g], recv_sem=r2.at[w, me], device_id={"factor": g}, device_id_type=MESH,
        )

    def arrived(place, sem, axis, source):
        pltpu.make_async_remote_copy(
            src_ref=place, dst_ref=place, send_sem=sem, recv_sem=sem, device_id={axis: source}, device_id_type=MESH
        ).wait_recv()

    loop(15, lambda j: copy_x(peer(j, 1), 0).start())

    loop(15, lambda j: copy_w(peer(j, 1)).start())
    for w in range(1, PARTS):
        loop(15, lambda j: copy_x(peer(j, 1), w).start())
    wbin[me] = wmsg[mine]
    for w in range(PARTS):
        inb[w, pl.ds(8 * UP * me, 8 * UP), :] = outa[mine, 8 * UP * w : 8 * UP * w + 8 * UP, :]

    def column_ones(n):
        chosen = lax.rem(lax.broadcasted_iota(jnp.int32, (256, 128), 1), 8) == n
        ebc[n] = jnp.where(chosen, 1.0, 0.0).astype(BF16)

    loop(8, column_ones)

    loads[3].wait()

    def order_targets(u):
        for k in range(8):
            rows = tgt[pl.ds(128 * u + 16 * k, 16), :].astype(F32)
            p = rev_const(k, 3)
            ts[u, pl.ds(p, 8, stride=8), :] = rows[0:8]
            ts[u, pl.ds(64 + p, 8, stride=8), :] = rows[8:16]

    loop(8, order_targets)

    loop(15, lambda j: arrived(wbin.at[peer(j, -1)], r1.at[peer(j, -1)], "factor", peer(j, -1)))
    wflat = wbin[...].reshape(128, 128)
    wtb[0:128, :] = wflat
    wtb[128:256, :] = wflat.T

    def spread_b(u):
        for s in range(3):
            for h in range(2):
                rows = pltpu.roll(wtb[64 * h + s : 64 * h + s + 57 : 8, :], lax.rem(128 - u, 128), axis=1)
                for kind in range(2):
                    for p in range(8):
                        k = 64 * kind + 8 * p
                        w1[kind, s, u, 2 * p + h] = jnp.broadcast_to(rows[:, k : k + 1], (8, 128))
        for kind in range(2):
            rows = wtb[pl.ds(128 + 64 * kind + u, 8, stride=8), :]
            for s in range(4):
                for f in range(16):
                    k = 8 * f + 4 + s
                    w2[kind, s, u, f] = jnp.broadcast_to(rows[:, k : k + 1], (8, 128))

    def side_b(w, k):
        u = UP * w + k
        x = [inb[w, pl.ds(64 * UP * h + 8 * k + p, 8, stride=8 * UP), :] for p in range(8) for h in range(2)]
        for s in range(3):
            for i in range(16):
                f1[s, u, i] = x[i]
            x = forward_pairs(x, 2 ** (s + 1), lambda i: w1[0, s, u, i], lambda i: w1[1, s, u, i])
        for i in range(16):
            f2[0, u, pl.ds(64 * (i % 2) + i // 2, 8, stride=8), :] = x[i]
        x = [f2[0, u, tile(f), :] for f in range(16)]
        for s in range(4):
            if s > 0:
                for f in range(16):
                    f2[s, u, tile(f), :] = x[f]
            x = forward_pairs(x, 2**s, lambda f: w2[0, s, u, f], lambda f: w2[1, s, u, f])
        b = []
        for f in range(16):
            place = tile(rev_const(f, 4))
            error = x[f] - ts[u, place, :]
            es[u, place, :] = error
            b.append((2.0 / TOKENS) * error)
        for s in range(3, -1, -1):
            for f in range(16):
                b2[s, u, tile(f), :] = b[f]
            b = backward_pairs(b, 2**s, lambda f: w2[0, s, u, f], lambda f: w2[1, s, u, f])
        for f in range(16):
            b2[4, u, tile(f), :] = b[f]
        b = [b2[4, u, pl.ds(64 * h + p, 8, stride=8), :] for p in range(8) for h in range(2)]
        for s in range(2, -1, -1):
            for i in range(16):
                b1[s, u, i] = b[i]
            b = backward_pairs(b, 2 ** (s + 1), lambda i: w1[0, s, u, i], lambda i: w1[1, s, u, i])
        for i in range(16):
            outb[w, pl.ds(64 * UP * (i % 2) + 8 * k + i // 2, 8, stride=8 * UP), :] = b[i]

    def copy_b(f, w):
        return pltpu.make_async_remote_copy(
            src_ref=outb.at[w, pl.ds(8 * UP * f, 8 * UP)], dst_ref=ina.at[mine, pl.ds(8 * UP * w, 8 * UP)],
            send_sem=s3.at[w, f], recv_sem=r3.at[w, mine], device_id={"factor": f}, device_id_type=MESH,
        )

    def part_b(w):
        loop(UP, lambda k: spread_b(UP * w + k), 2)
        loop(
            15,
            lambda j: arrived(
                inb.at[w, pl.ds(8 * UP * peer(14 - j, -1), 8 * UP)], r2.at[w, peer(14 - j, -1)], "factor", peer(14 - j, -1)
            ),
        )
        loop(UP, lambda k: side_b(w, k), 2)
        loop(15, lambda j: copy_b(peer(j, 1), w).start())
        ina[mine, pl.ds(8 * UP * w, 8 * UP), :] = outb[w, pl.ds(8 * UP * me, 8 * UP), :]

    loop(PARTS, part_b)

    def order_errors(u):
        for k in range(8):
            p = rev_const(k, 3)
            for h in range(2):
                res[pl.ds(128 * u + 16 * k + 8 * h, 8), :] = es[u, pl.ds(64 * h + p, 8, stride=8), :]

    loop(8, order_errors)

    def grads_high(u):
        total = None
        for s in range(4):
            blocks = [
                b2[s, u, tile(f), :] * f2[s, u, tile(f ^ 2**s if kind else f), :] for kind in range(2) for f in range(16)
            ]
            term = lane_sums(blocks, 4 + s)
            total = term if total is None else total + term
        for kind in range(2):
            gz[pl.ds(64 * kind + u, 8, stride=8), :] = choose(tiles_of(total, kind))

    loop(8, grads_high)
    gt[...] = gz[...].T
    partb[...] = jnp.zeros_like(partb)

    def grads_low(u):
        for s in range(3):
            blocks = [
                b1[s, u, 2 * p + h] * f1[s, u, 2 * (p ^ 2**s if kind else p) + h]
                for h in range(2) for kind in range(2) for p in range(8)
            ]
            sums = lane_sums(blocks, u)
            for h in range(2):
                partb[s, h] = partb[s, h] + choose(tiles_of(sums, h))

    loop(8, grads_low)
    for s in range(3):
        for h in range(2):
            gt[64 * h + s : 64 * h + s + 57 : 8, :] = partb[s, h]

    def copy_g(f):
        return pltpu.make_async_remote_copy(
            src_ref=gt.at[pl.ds(8 * f, 8)], dst_ref=gin.at[pl.ds(8 * mine, 8)],
            send_sem=s4.at[f], recv_sem=r4.at[mine], device_id={"factor": f}, device_id_type=MESH,
        )

    loop(15, lambda j: copy_g(peer(j, 1)).start())
    gin[pl.ds(8 * mine, 8), :] = gt[pl.ds(8 * me, 8), :]

    def drain_first(j):
        g = peer(j, 1)
        copy_w(g).wait_send()
        for w in range(PARTS):
            copy_x(g, w).wait_send()

    loop(15, drain_first)

    def arrived_a(w):
        loop(
            15,
            lambda j: arrived(
                ina.at[rev4(peer(14 - j, -1)), pl.ds(8 * UP * w, 8 * UP)], r3.at[w, rev4(peer(14 - j, -1))],
                "factor", peer(14 - j, -1),
            ),
        )

    def level_a(s, u0):
        u1 = u0 + 2 ** (6 - s)
        rows = [pl.ds(8 * u0, 8), pl.ds(8 * u1, 8)]
        source = ina if s == 6 else b5.at[6 - s - 1]
        b = [[source[a, r, :] for r in rows] for a in range(16)]
        blocks = [
            b[a][k] * fa[s, a, rows[k ^ kind], :] for k in range(2) for kind in range(2) for a in range(16)
        ]
        sums = lane_sums(blocks, s)
        for k, u in ((0, u0), (1, u1)):
            for kind in range(2):
                term = choose(tiles_of(sums, 2 * k + kind))
                parta[kind, u] = term if s == 6 else parta[kind, u] + term
        for a in range(16):
            for k in range(2):
                b5[6 - s, a, rows[k], :] = (
                    wa[0, s, a, rows[k], :] * b[a][k] + wa[1, s, a, rows[1 - k], :] * b[a][1 - k]
                )

    for w in range(PARTS):
        arrived_a(w)
        if UP == 2:
            level_a(6, 2 * w)
            if w % 2 == 1:
                loop(2, lambda k: level_a(5, 2 * w - 2 + k), 2)
        else:
            loop(UP // 2, lambda k: level_a(6, UP * w + 2 * k))
            loop(UP // 2, lambda k: level_a(5, UP * w + 4 * lax.div(k, 2) + lax.rem(k, 2)))
    loop(4, lambda k: level_a(4, k), 4)

    def last_a(u):
        here = pl.ds(8 * u, 8)
        b = [b5[2, a, here, :] for a in range(16)]
        total = None
        for s in range(3, -1, -1):
            blocks = [b[a] * fa[s, a ^ (kind * 2**s), here, :] for kind in range(2) for a in range(16)]
            term = lane_sums(blocks, s)
            total = term if total is None else total + term
            if s > 0:
                b = backward_pairs(b, 2**s, lambda a: wa[0, s, a, here, :], lambda a: wa[1, s, a, here, :])
        for kind in range(2):
            gpart[pl.ds(128 * kind + u, 8, stride=16), :] = parta[kind, u] + choose(tiles_of(total, kind))

    loop(8, last_a, 8)

    loop(15, lambda j: arrived(gin.at[pl.ds(8 * rev4(peer(j, -1)), 8)], r4.at[rev4(peer(j, -1))], "factor", peer(j, -1)))
    turned = gin[...].T
    for c in range(16):
        gpart[16 * c + 8 : 16 * c + 16, :] = turned[8 * c : 8 * c + 8]

    def copy_r(c):
        return pltpu.make_async_remote_copy(
            src_ref=gpart.at[pl.ds(16 * c, 16)], dst_ref=rs.at[col], send_sem=s5.at[c], recv_sem=r5.at[col],
            device_id={"col": c}, device_id_type=MESH,
        )

    def other(j):
        return lax.rem(col + 1 + j, 16)

    loop(15, lambda j: copy_r(other(j)).start())
    rs[col] = gpart[pl.ds(16 * col, 16), :]
    def drain_second(j):
        g = peer(j, 1)
        copy_g(g).wait_send()
        for w in range(PARTS):
            copy_b(g, w).wait_send()

    loop(15, drain_second)
    loop(15, lambda j: arrived(rs.at[other(j)], r5.at[other(j)], "col", other(j)))
    terms = [rs[c] for c in range(16)]
    while len(terms) > 1:
        terms = [terms[i] + terms[i + 1] for i in range(0, len(terms), 2)]
    gs[...] = terms[0]
    row_a = lax.rem(lax.broadcasted_iota(jnp.int32, (128, 128), 0), 16)
    lanes = lax.broadcasted_iota(jnp.int32, (128, 128), 1)
    out_row = lax.broadcasted_iota(jnp.int32, (16, 128), 0)
    out_lane = lax.broadcasted_iota(jnp.int32, (16, 128), 1)
    place = lax.rem(out_lane, 8)
    level_of = [place, 7 + place - jnp.where(place > 3, 1, 0)]
    valid = [place != 7, place != 3]
    own_a = lax.div(lanes, 8) == row_a
    total = jnp.zeros((16, 128), F32)
    for k in range(2):
        wide = jnp.concatenate(
            [jnp.broadcast_to(gs[8 * k + rev_const(t, 3) : 8 * k + rev_const(t, 3) + 1, :], (16, 128)) for t in range(8)], axis=0
        )
        wide = jnp.where(own_a, wide, 0.0)
        pick = jnp.where((level_of[k] == out_row) & valid[k], 1.0, 0.0).astype(BF16)
        for part in thirds(wide):
            total = total + lax.dot_general(
                pick, part.astype(BF16), (((1,), (1,)), ((), ())), preferred_element_type=F32
            )
    kind = lax.div(col, 8)
    here = pl.ds(pl.multiple_of(128 * lax.rem(col, 8), 128), 128)
    weights = jnp.where(kind == 0, dg[:, here], cr[:, here])
    gout[col, 0:14] = weights - step_scale * total[0:14]

    def copy_s(c):
        return pltpu.make_async_remote_copy(
            src_ref=gout.at[col], dst_ref=gout.at[col], send_sem=s6.at[c], recv_sem=r6.at[col],
            device_id={"col": c}, device_id_type=MESH,
        )

    loop(15, lambda j: copy_s(other(j)).start())
    loop(15, lambda j: copy_r(other(j)).wait_send())
    loop(15, lambda j: arrived(gout.at[other(j)], r6.at[other(j)], "col", other(j)))
    for p in range(8):
        nd[:, 128 * p : 128 * p + 128] = gout[p, 0:14]
        nc[:, 128 * p : 128 * p + 128] = gout[8 + p, 0:14]

    loop(15, lambda j: copy_s(other(j)).wait_send())


def write_out(a0, a1, a2, o0, o1, o2, sem):
    copies = [pltpu.make_async_copy(a, o, sem.at[k]) for k, (a, o) in enumerate([(a2, o2), (a0, o0), (a1, o1)])]
    for copy in copies:
        copy.start()
    for copy in copies:
        copy.wait()


def per_device(activations, targets, diagonal, crossing):
    height, width = activations.shape
    plain = lambda *shape: pltpu.VMEM(shape, F32)
    sems = lambda *shape: pltpu.SemaphoreType.DMA(shape)
    vmem, anywhere = pl.BlockSpec(memory_space=pltpu.VMEM), pl.BlockSpec(memory_space=pl.ANY)
    shapes = (diagonal.shape, crossing.shape, (height, width))
    results = pl.pallas_call(
        kernel,
        out_shape=tuple(pltpu.VMEM(shape, F32) for shape in shapes),
        in_specs=[anywhere] * 4,
        out_specs=(vmem,) * 3,
        scratch_shapes=[
            pltpu.VMEM((1024, 128), BF16), pltpu.VMEM((1024, 128), BF16),
            plain(14, 1024), plain(14, 1024),
            plain(1024, 128), plain(8, 128, 128), plain(8, 128, 128), plain(128, 1024), plain(1024, 128),
            pltpu.VMEM((7, 128, 256), BF16), pltpu.VMEM((8, 256, 128), BF16), plain(128, 128), plain(16, 8, 128), plain(16, 8, 128),
            plain(256, 128),
            plain(2, 7, 16, 64, 128), plain(2, 3, 8, 16, 8, 128), plain(2, 4, 8, 16, 8, 128),
            plain(7, 16, 64, 128), plain(3, 16, 64, 128),
            plain(3, 8, 16, 8, 128), plain(4, 8, 128, 128), plain(3, 8, 16, 8, 128), plain(5, 8, 128, 128),
            plain(16, 64, 128), plain(PARTS, 128 * UP, 128), plain(PARTS, 128 * UP, 128), plain(16, 64, 128),
            plain(2, 8, 8, 128), plain(3, 2, 8, 128), plain(128, 128), plain(128, 128), plain(128, 128),
            plain(256, 128), plain(16, 16, 128), plain(16, 128), plain(16, 16, 128),
            sems(4),
            sems(16), sems(16), sems(PARTS, 16), sems(PARTS, 16), sems(PARTS, 16), sems(PARTS, 16),
            sems(16), sems(16), sems(16), sems(16), sems(16), sems(16),
        ],
        compiler_params=pltpu.CompilerParams(
            collective_id=0, has_side_effects=True, vmem_limit_bytes=56 * 2**20
        ),
    )(activations, targets, diagonal, crossing)
    return pl.pallas_call(
        write_out,
        out_shape=tuple(jax.ShapeDtypeStruct(shape, F32) for shape in shapes),
        in_specs=[anywhere] * 3,
        out_specs=(anywhere,) * 3,
        scratch_shapes=[sems(3)],
        compiler_params=pltpu.CompilerParams(vmem_limit_bytes=2**20),
    )(*results)


def solution(mesh):
    placed = (P("factor", "col"), P("factor", "col"), P(None, "factor"), P(None, "factor"))
    return jax.shard_map(
        per_device,
        mesh=mesh,
        in_specs=placed,
        out_specs=(P(None, "factor"), P(None, "factor"), P("factor", "col")),
        check_vma=False,
    )
```
